512 devices in a mesh: ctx: 64 (over y_lo, z, core), mp: 8 (over y_hi, x).
Axes of the slice: x: 4, y: 4 (y_hi: 2, y_lo: 2; y = y_hi * 2 + y_lo), z: 16, core: 2. Of those that a mesh axis runs over, the one named last changes fastest.
Arguments:
- byte_states: bfloat16 [1024, 4096], P('mp', 'ctx'), may hold values from -6 to 6
- shorten_weight: bfloat16 [4, 64, 8, 8, 8192], P(None, None, 'mp', None, 'ctx'), may hold values from -1 to 1
- norm_gain: float32 [8192], P('ctx'), may hold values from 0.1 to 1.9
- qkv_weight: bfloat16 [64, 8, 16, 3, 8192], P(None, 'mp', None, None, 'ctx'), may hold values from -0.0625 to 0.0625
- qk_gain: float32 [2, 128], replicated, may hold values from 0.1 to 1.9
- out_weight: bfloat16 [64, 8, 16, 8192], P(None, 'mp', None, 'ctx'), may hold values from -0.375 to 0.375
- up_weight: bfloat16 [64, 8, 16, 4, 4096], P(None, 'mp', None, None, 'ctx'), may hold values from -0.0625 to 0.0625
- doc_lengths: int32 [6], replicated, may hold values from 1 to 768, 1024 in all
Outputs:
- byte_out: bfloat16 [1024, 4096], P('mp', 'ctx')
The draws below stay inside these ranges and needn't reach their ends.
Inputs may be any that keep to these rules, and one draw needn't show every extreme that they name: `doc_lengths`: the lengths are positive and sum to 1024; the largest equals 768.
All inputs are finite; a program needn't handle non-finite values.
Results may differ from the reference program's by a relative error of at most 0.04.
Values may be sent and summed in bfloat16 or wider, within the bound.
A program may use at most 64 MiB of HBM per device.

```python
import math
import jax
import jax.numpy as jnp
import numpy as np
from jax import lax

D = 4096
E = 8192
HD = 128
HEADS = 64
SHORT_ROWS = 256
BYTES = 1024
NDOC = 6
DPIECE = 8
EPIECE = 16
N_CTX = 64
N_MP = 8


def column_scales(key, rise):
    column_pos = jnp.arange(E, dtype=jnp.float32) / (E - 1)
    rough = jnp.exp(jax.random.uniform(key, (E,), jnp.float32, math.log(0.7), math.log(1.4)))
    mean_square = (rise * rise - 1.0) / (2.0 * math.log(rise))
    return jnp.exp(column_pos * math.log(rise)) * rough / math.sqrt(mean_square)


def draw_shorten_weight(key, part):
    key = jax.random.fold_in(key, 11)
    key_base, key_cols = jax.random.split(key)
    shape = (4, N_CTX, N_MP, DPIECE, E)
    base = jnp.clip(jax.random.normal(key_base, shape, jnp.float32), -6.0, 6.0)
    scales = column_scales(key_cols, 3.0)
    return (base * scales / math.sqrt(4.0 * D)).astype(jnp.bfloat16)


def levels(stream_key, shape, cuts, least, high):
    gain = 1.0
    for dim, parts in cuts:
        draws = jax.random.uniform(jax.random.fold_in(jax.random.fold_in(stream_key, 6), dim), (parts,), jnp.float32, least / len(cuts), high / len(cuts))
        gain = gain * jnp.repeat(jnp.exp(draws), shape[dim] // parts).reshape((-1,) + (1,) * (len(shape) - 1 - dim))
    return gain


def length_profile(amount, total, most, lean):
    portions = [(1 << 20) // math.isqrt(grade ** lean) + 1 for grade in range(2, amount + 1)]
    surplus, counts = total - most - (amount - 1), [1] * (amount - 1)
    while surplus > 0:
        free = [i for i in range(amount - 1) if counts[i] < most]
        pool, budget = sum([portions[i] for i in free]), surplus
        for i in free:
            addition = min(most - counts[i], max(1, budget * portions[i] // pool), surplus)
            counts[i] = counts[i] + addition
            surplus = surplus - addition
    return np.array([most] + counts)


def uneven(stream_key, amount, total, bound, lean):
    if amount == 2:
        one = jax.random.randint(stream_key, (), max(1, total - bound), min(bound, total - 1) + 1)
        return jnp.stack([one, total - one])
    tallies = jnp.asarray(length_profile(amount, total, bound, lean), jnp.int32)
    pairs = (amount - 1) // 2
    donor, receiver = tallies[1:1 + 2 * pairs:2], tallies[2:2 + 2 * pairs:2]
    room = jnp.minimum(donor - 1, bound - receiver)
    shifted = jax.random.randint(jax.random.fold_in(stream_key, 1), (pairs,), 0, 1 << 20) % (room + 1)
    tallies = tallies.at[1:1 + 2 * pairs:2].set(donor - shifted).at[2:2 + 2 * pairs:2].set(receiver + shifted)
    return tallies[jax.random.permutation(jax.random.fold_in(stream_key, 2), amount)]


def normal_values(rng, dims, deviation, most, cuts=(), kind=jnp.bfloat16):
    result = deviation * jax.random.normal(rng, dims, jnp.float32)
    if cuts:
        result = result * levels(rng, dims, cuts, -0.22, 0.18)
    return jnp.clip(result, -most, most).astype(kind)


def setup_inputs(seed: int = 0) -> dict:
    seeds = jax.random.split(jax.random.key(seed), 9)
    return {
        "byte_states": normal_values(seeds[0], (BYTES, D), 1.0, 6.0, ((0, 8), (1, 64))),
        "shorten_weight": draw_shorten_weight(jax.random.fold_in(seeds[8], 71), 0),
        "norm_gain": jnp.clip(1.0 + 0.18 * jax.random.normal(seeds[2], (E,), jnp.float32), 0.1, 1.9),
        "qkv_weight": normal_values(seeds[3], (N_CTX, N_MP, EPIECE, 3, E), E ** -0.5, 0.0625, ((1, 8), (4, 64))),
        "qk_gain": jnp.clip(1.0 + 0.18 * jax.random.normal(seeds[4], (2, HD), jnp.float32), 0.1, 1.9),
        "out_weight": normal_values(seeds[5], (N_CTX, N_MP, EPIECE, E), (E // 32) ** -0.5, 0.375, ((1, 8), (3, 64))),
        "up_weight": normal_values(seeds[6], (N_CTX, N_MP, EPIECE, 4, D), E ** -0.5, 0.0625, ((1, 8), (4, 64))),
        "doc_lengths": uneven(seeds[7], NDOC, BYTES, 3 * BYTES // 4, 1).astype(jnp.int32),
    }


def head_norm(values_in, gain_row):
    inverse = lax.rsqrt(lax.optimization_barrier(jnp.mean(values_in * values_in, axis=-1, keepdims=True)) + 1e-06)
    return values_in * inverse * gain_row

def reference(byte_states, shorten_weight, norm_gain, qkv_weight, qk_gain, out_weight, up_weight, doc_lengths):
    padded = jnp.pad(byte_states, ((3, 0), (0, 0)))[:BYTES]
    stacked = padded.reshape(SHORT_ROWS, 4 * D)
    shortened = jnp.dot(stacked, shorten_weight.reshape(4 * D, E), preferred_element_type=jnp.float32).astype(jnp.bfloat16)
    short_wide = shortened.astype(jnp.float32)
    inverse = lax.rsqrt(lax.optimization_barrier(jnp.mean(short_wide * short_wide, axis=1, keepdims=True)) + 1e-06)
    normed = (short_wide * inverse * norm_gain.astype(jnp.float32)[None, :]).astype(jnp.bfloat16)
    projected = jnp.dot(normed, qkv_weight.reshape(E, 3 * E), preferred_element_type=jnp.float32)
    triple = projected.reshape(SHORT_ROWS, 3, HEADS, HD)
    queries = head_norm(triple[:, 0], qk_gain[0].astype(jnp.float32)).astype(jnp.bfloat16)
    key_rows = head_norm(triple[:, 1], qk_gain[1].astype(jnp.float32)).astype(jnp.bfloat16)
    values = triple[:, 2].astype(jnp.bfloat16)
    doc_ends = jnp.cumsum(doc_lengths).astype(jnp.int32)
    positions = 4 * jnp.arange(SHORT_ROWS, dtype=jnp.int32)
    segment = lax.optimization_barrier(jnp.sum((doc_ends[None, :] <= positions[:, None]).astype(jnp.int32), axis=1)).astype(jnp.int32)
    row_index = jnp.arange(SHORT_ROWS, dtype=jnp.int32)
    allowed = (row_index[None, :] <= row_index[:, None]) & (segment[None, :] == segment[:, None])
    query_wide = lax.optimization_barrier(queries).astype(jnp.float32)
    key_wide = lax.optimization_barrier(key_rows).astype(jnp.float32)
    value_wide = lax.optimization_barrier(values).astype(jnp.float32)
    scores = jnp.einsum('qhd,khd->hqk', query_wide, key_wide) * (1.0 / HD ** 0.5)
    weights = jnp.where(allowed[None, :, :], jnp.exp(scores), 0.0)
    denominator = lax.optimization_barrier(jnp.sum(weights, axis=2))
    rounded = lax.optimization_barrier(weights.astype(jnp.bfloat16)).astype(jnp.float32)
    numerator = jnp.einsum('hqk,khd->hqd', rounded, value_wide)
    attended = (numerator / denominator[:, :, None]).transpose(1, 0, 2).reshape(SHORT_ROWS, E).astype(jnp.bfloat16)
    mixed_proj = jnp.dot(attended, out_weight.reshape(E, E), preferred_element_type=jnp.float32)
    hidden = (short_wide + mixed_proj).astype(jnp.bfloat16)
    upward = jnp.dot(hidden, up_weight.reshape(E, 4 * D), preferred_element_type=jnp.float32).reshape(BYTES, D)
    return (byte_states.astype(jnp.float32) + upward).astype(jnp.bfloat16)
```

```python
import jax
import jax.numpy as jnp
from jax import lax
from jax.experimental import pallas as pl
from jax.experimental.pallas import tpu as pltpu
from jax.sharding import PartitionSpec as P

F32 = jnp.float32
BF16 = jnp.bfloat16
MESH = pl.DeviceIdType.MESH
ROWS = 256
PLANE = 32
DEPTH = 16
SLOTS = 4


def dot00(a, b):
    return lax.dot_general(a, b, (((0,), (0,)), ((), ())), preferred_element_type=F32)


def kernel(
    bytes_ref, wconv_hbm, gain_ref, wqkv_hbm, qk_gain_ref, wout_hbm, wup_hbm, docs_ref,
    out_ref,
    p0_wide, p0_send, p0_recv,
    x1, x2, x3, x4,
    gains, gain_own,
    wconv_in, wqkv_in, wout_in, wup_in,
    wconv_t, wqk, wv_t, wout_t,
    s_conv, s_qk, s_v, s_out, s_up, s_sq,
    r_conv, r_qk, r_v, r_out, r_up, r_sq,
    short_own, qk_all, out_wide,
    send_sem, recv_sem, local_sem,
):
    ctx = lax.axis_index("ctx")
    mp = lax.axis_index("mp")
    y_lo, z, core = lax.div(ctx, 32), lax.rem(lax.div(ctx, 2), DEPTH), lax.rem(ctx, 2)
    y, x = lax.div(mp, 4) * 2 + y_lo, lax.rem(mp, 4)
    slot = y_lo * 2 + core
    me = mp * SLOTS + slot

    def plane_peer(i):
        def offset(k):
            return jnp.where(k == 3, 0, jnp.where(k == 2, 3, 2 - k))

        px = lax.rem(x + offset(lax.div(i, 8)), 4)
        py = lax.rem(y + offset(lax.rem(lax.div(i, 2), 4)), 4)
        pc = lax.rem(core + 1 + lax.rem(i, 2), 2)
        p_lo = lax.rem(py, 2)
        return (p_lo * 32 + z * 2 + pc, lax.div(py, 2) * 4 + px), p_lo * 2 + pc

    def depth_peer(i):
        far = 8 - lax.div(i + 1, 2)
        step = jnp.where(lax.rem(i, 2) == 1, far, DEPTH - far)
        pz = lax.rem(z + step, DEPTH)
        return (y_lo * 32 + pz * 2 + core, mp)

    def loop(count, body):
        def step(i, carry):
            body(i)
            return carry

        lax.fori_loop(0, count, step, 0)

    def put(src, dst, sem, device):
        pltpu.make_async_remote_copy(
            src_ref=src, dst_ref=dst, send_sem=send_sem.at[sem], recv_sem=recv_sem.at[sem],
            device_id=device, device_id_type=MESH,
        ).start()

    def arrived(view, sem):
        pltpu.make_async_copy(view, view, recv_sem.at[sem]).wait()

    def left(view, sem):
        pltpu.make_async_copy(view, view, send_sem.at[sem]).wait()

    def along_depth(buf, sem):
        loop(DEPTH - 1, lambda i: put(buf.at[z], buf.at[z], sem, depth_peer(i)))

    def to_plane(piece, dst, sem):
        def body(i):
            device, its_slot = plane_peer(i)
            put(piece(its_slot, device[1]), dst.at[me], sem, device)

        loop(PLANE - 1, body)

    barrier = pltpu.get_barrier_semaphore()
    loop(
        DEPTH - 1,
        lambda i: pl.semaphore_signal(
            barrier, inc=1, device_id=depth_peer(i), device_id_type=MESH
        ),
    )
    loop(
        PLANE - 1,
        lambda i: pl.semaphore_signal(
            barrier, inc=1, device_id=plane_peer(i)[0], device_id_type=MESH
        ),
    )

    own = []
    for tap in range(4):
        own.append((wconv_hbm.at[tap, y_lo, :, core], wconv_in.at[slot, :, tap]))
    for src, dst in ((wqkv_hbm, wqkv_in), (wout_hbm, wout_in), (wup_hbm, wup_in)):
        own.append((src.at[y_lo, :, core], dst.at[slot]))
    own = [pltpu.make_async_copy(a, b, local_sem.at[i]) for i, (a, b) in enumerate(own)]
    for copy in own:
        copy.start()

    local = bytes_ref[...]
    row = lax.broadcasted_iota(jnp.int32, (128, ROWS), 0)
    col = lax.broadcasted_iota(jnp.int32, (128, ROWS), 1)
    for tap in range(4):
        pick = (row + mp * 128 == 4 * col + (tap - 3)).astype(F32).astype(BF16)
        placed = dot00(local, pick)
        for m in range(8):
            p0_wide[m, tap * 8 : tap * 8 + 8, :] = placed[m * 8 : m * 8 + 8, :]
    p0_send[...] = p0_wide[...].astype(BF16)
    p0_recv[mp] = p0_send[mp]

    lane = lax.broadcasted_iota(jnp.int32, (16, 128), 1)
    feat = lax.broadcasted_iota(jnp.int32, (16, 128), 0)
    mine = jnp.where(lane == feat + mp * 16, gain_ref[...], 0.0)
    gain_own[...] = jnp.broadcast_to(jnp.sum(mine, axis=1, keepdims=True), (16, 128))
    gains[z] = gain_own[...]

    pl.semaphore_wait(barrier, DEPTH - 1 + PLANE - 1)

    def trade(i):
        other = lax.rem(mp + 1 + i, 8)
        put(p0_send.at[other], p0_recv.at[mp], 0, (ctx, other))

    loop(7, trade)

    peers = []
    for step in range(1, SLOTS):
        p_lo = lax.rem(y_lo + step // 2, 2)
        p_core = lax.rem(core + step % 2, 2)
        peers.append((p_lo, p_core, (p_lo * 32 + z * 2 + p_core, mp)))
    for p_lo, p_core, device in peers:
        for tap in range(4):
            put(wconv_hbm.at[tap, p_lo, :, p_core], wconv_in.at[slot, :, tap], 1, device)
    for src, dst, sem in ((wqkv_hbm, wqkv_in, 2), (wout_hbm, wout_in, 3), (wup_hbm, wup_in, 4)):
        for p_lo, p_core, device in peers:
            put(src.at[p_lo, :, p_core], dst.at[slot], sem, device)

    arrived(p0_recv.at[pl.ds(0, 7)], 0)
    block = p0_recv[0].astype(F32)
    for m in range(1, 8):
        block = block + p0_recv[m].astype(F32)
    x1[z] = block.astype(BF16)
    along_depth(x1, 5)
    loop(DEPTH - 1, lambda i: put(gain_own, gains.at[z], 6, depth_peer(i)))

    for copy in own[:4]:
        copy.wait()
    arrived(wconv_in.at[pl.ds(0, 3)], 1)
    for s in range(SLOTS):
        flat = wconv_in[s].astype(F32).reshape(DEPTH * 32, 128)
        wconv_t[s * 128 : s * 128 + 128, :] = flat.T.astype(BF16)

    arrived(x1.at[pl.ds(0, 15)], 5)
    conv = jnp.dot(
        wconv_t[...], x1[...].reshape(DEPTH * 32, ROWS), preferred_element_type=F32
    )
    s_conv[...] = conv.astype(BF16).reshape(SLOTS, 128, ROWS)

    def feature_piece(buf):
        return lambda its_slot, m: buf.at[its_slot, pl.ds(pl.multiple_of(m * 16, 16), 16), :]

    def row_piece(buf):
        return lambda its_slot, m: buf.at[its_slot, pl.ds(pl.multiple_of(m * 32, 32), 32), :]

    to_plane(feature_piece(s_conv), r_conv, 7)
    r_conv[me] = s_conv[slot, pl.ds(pl.multiple_of(mp * 16, 16), 16), :]

    own[4].wait()
    arrived(wqkv_in.at[pl.ds(0, 3)], 2)
    arrived(gains.at[pl.ds(0, 15)], 6)
    column = gains[...].reshape(256, 128)
    for s in range(SLOTS):
        w = wqkv_in[s].reshape(256, 384)
        for kind in range(2):
            wqk[:, s * 256 + kind * 128 : s * 256 + kind * 128 + 128] = (
                w[:, kind * 128 : kind * 128 + 128].astype(F32) * column
            ).astype(BF16)
        wv_t[s * 128 : s * 128 + 128, :] = (w[:, 256:].astype(F32) * column).T.astype(BF16)

    def total(buf):
        acc = buf[0].astype(F32)
        for i in range(1, PLANE):
            acc = acc + buf[i].astype(F32)
        return acc

    arrived(r_conv.at[pl.ds(0, 31)], 7)
    short = total(r_conv).astype(BF16)
    short_own[...] = short
    x2[z] = short
    along_depth(x2, 8)

    own[5].wait()
    arrived(wout_in.at[pl.ds(0, 3)], 3)
    for s in range(SLOTS):
        wout_t[s * 128 : s * 128 + 128, :] = wout_in[s].reshape(256, 128).astype(F32).T.astype(BF16)

    arrived(x2.at[pl.ds(0, 15)], 8)
    gathered = x2[...].reshape(256, ROWS)
    wide = gathered.astype(F32)
    squares = jnp.sum(wide * wide, axis=0, keepdims=True)
    s_sq[0:1, :] = squares[:, :128]
    s_sq[1:2, :] = squares[:, 128:]
    r_sq[me] = s_sq[...]
    qk = dot00(gathered, wqk[...])
    for s in range(SLOTS):
        s_qk[s] = qk[:, s * 256 : s * 256 + 256].astype(BF16)
    to_plane(row_piece(s_qk), r_qk, 9)
    to_plane(lambda its_slot, m: s_sq, r_sq, 10)
    v = jnp.dot(wv_t[...], gathered, preferred_element_type=F32)
    s_v[...] = v.astype(BF16).reshape(SLOTS, 128, ROWS)
    to_plane(feature_piece(s_v), r_v, 11)
    r_qk[me] = s_qk[slot, pl.ds(pl.multiple_of(mp * 32, 32), 32), :]
    r_v[me] = s_v[slot, pl.ds(pl.multiple_of(mp * 16, 16), 16), :]

    key = lax.broadcasted_iota(jnp.int32, (ROWS, ROWS), 0)
    query = lax.broadcasted_iota(jnp.int32, (ROWS, ROWS), 1)
    key_pos = lax.broadcasted_iota(jnp.int32, (ROWS, 1), 0) * 4
    query_pos = lax.broadcasted_iota(jnp.int32, (1, ROWS), 1) * 4
    key_seg = jnp.zeros((ROWS, 1), jnp.int32)
    query_seg = jnp.zeros((1, ROWS), jnp.int32)
    end = jnp.int32(0)
    for d in range(docs_ref.shape[0]):
        end = end + docs_ref[d]
        key_seg = key_seg + (key_pos >= end).astype(jnp.int32)
        query_seg = query_seg + (query_pos >= end).astype(jnp.int32)
    allowed = (key <= query) & (key_seg == query_seg)

    arrived(r_sq.at[pl.ds(0, 31)], 10)
    mean = jnp.sum(r_sq[...], axis=0) / 8192.0
    inverse = lax.rsqrt(mean + 1e-06)
    inverse = jnp.concatenate([inverse[0:1, :], inverse[1:2, :]], axis=1)
    at_row = lax.broadcasted_iota(jnp.int32, (32, ROWS), 0) + mp * 32
    at_lane = lax.broadcasted_iota(jnp.int32, (32, ROWS), 1)
    row_inverse = jnp.sum(jnp.where(at_row == at_lane, inverse, 0.0), axis=1, keepdims=True)

    arrived(r_qk.at[pl.ds(0, 31)], 9)
    both = total(r_qk) * row_inverse
    for kind in range(2):
        part = both[:, kind * 128 : kind * 128 + 128]
        scale = lax.rsqrt(jnp.mean(part * part, axis=1, keepdims=True) + 1e-06)
        qk_all[mp, :, kind * 128 : kind * 128 + 128] = (
            part * scale * qk_gain_ref[kind : kind + 1, :]
        ).astype(BF16)

    def share(i):
        other = lax.rem(mp + 1 + i, 8)
        put(qk_all.at[mp], qk_all.at[mp], 12, (ctx, other))

    loop(7, share)

    arrived(r_v.at[pl.ds(0, 31)], 11)
    values = (total(r_v) * inverse).astype(BF16)

    arrived(qk_all.at[pl.ds(0, 7)], 12)
    queries = qk_all[:, :, 0:128].reshape(ROWS, 128)
    keys = qk_all[:, :, 128:256].reshape(ROWS, 128)
    scores = lax.dot_general(
        keys, queries, (((1,), (1,)), ((), ())), preferred_element_type=F32
    ) * (1.0 / 128**0.5)
    weights = jnp.where(allowed, jnp.exp(scores), 0.0)
    denominator = jnp.sum(weights, axis=0, keepdims=True)
    numerator = jnp.dot(values, weights.astype(BF16), preferred_element_type=F32)
    x3[z] = (numerator / denominator).astype(BF16)
    along_depth(x3, 13)

    own[6].wait()
    arrived(wup_in.at[pl.ds(0, 3)], 4)

    arrived(x3.at[pl.ds(0, 15)], 13)
    mixed = jnp.dot(wout_t[...], x3[...].reshape(256, ROWS), preferred_element_type=F32)
    s_out[...] = mixed.astype(BF16).reshape(SLOTS, 128, ROWS)
    to_plane(feature_piece(s_out), r_out, 14)
    r_out[me] = s_out[slot, pl.ds(pl.multiple_of(mp * 16, 16), 16), :]
    arrived(r_out.at[pl.ds(0, 31)], 14)
    x4[z] = (short_own[...].astype(F32) + total(r_out)).astype(BF16)
    along_depth(x4, 15)
    arrived(x4.at[pl.ds(0, 15)], 15)
    hidden = x4[...].reshape(256, ROWS)
    for s in range(SLOTS):
        s_up[s] = dot00(hidden, wup_in[s].reshape(256, 256)).astype(BF16)
    to_plane(row_piece(s_up), r_up, 16)
    r_up[me] = s_up[slot, pl.ds(pl.multiple_of(mp * 32, 32), 32), :]

    left(p0_recv.at[pl.ds(0, 7)], 0)
    left(wconv_in.at[pl.ds(0, 3)], 1)
    left(wqkv_in.at[pl.ds(0, 3)], 2)
    left(wout_in.at[pl.ds(0, 3)], 3)
    left(wup_in.at[pl.ds(0, 3)], 4)
    left(x1.at[pl.ds(0, 15)], 5)
    left(gains.at[pl.ds(0, 15)], 6)
    left(r_conv.at[pl.ds(0, 31)], 7)
    left(x2.at[pl.ds(0, 15)], 8)
    left(r_qk.at[pl.ds(0, 31)], 9)
    left(r_sq.at[pl.ds(0, 31)], 10)
    left(r_v.at[pl.ds(0, 31)], 11)
    left(qk_all.at[pl.ds(0, 7)], 12)
    left(x3.at[pl.ds(0, 15)], 13)
    left(r_out.at[pl.ds(0, 31)], 14)
    left(x4.at[pl.ds(0, 15)], 15)

    arrived(r_up.at[pl.ds(0, 31)], 16)
    upward = total(r_up)
    for tap in range(4):
        out_wide[pl.ds(tap, 32, stride=4), :] = upward[:, tap * 64 : tap * 64 + 64]
    out_ref[...] = (bytes_ref[...].astype(F32) + out_wide[...]).astype(BF16)
    left(r_up.at[pl.ds(0, 31)], 16)


def per_device(
    byte_states, shorten_weight, norm_gain, qkv_weight, qk_gain, out_weight, up_weight, doc_lengths
):
    vmem = pl.BlockSpec(memory_space=pltpu.VMEM)
    hbm = pl.BlockSpec(memory_space=pl.ANY)
    smem = pl.BlockSpec(memory_space=pltpu.SMEM)

    def buf(*shape, dtype=BF16):
        return pltpu.VMEM(shape, dtype)

    return pl.pallas_call(
        kernel,
        out_shape=jax.ShapeDtypeStruct(byte_states.shape, BF16),
        in_specs=[vmem, hbm, vmem, hbm, vmem, hbm, hbm, smem],
        out_specs=vmem,
        scratch_shapes=[
            buf(8, 32, ROWS, dtype=F32),
            buf(8, 32, ROWS),
            buf(8, 32, ROWS),
            buf(DEPTH, 32, ROWS),
            buf(DEPTH, 16, ROWS),
            buf(DEPTH, 16, ROWS),
            buf(DEPTH, 16, ROWS),
            buf(DEPTH, 16, 128, dtype=F32),
            buf(16, 128, dtype=F32),
            buf(SLOTS, DEPTH, 4, 8, 128),
            buf(SLOTS, DEPTH, 16, 384),
            buf(SLOTS, DEPTH, 16, 128),
            buf(SLOTS, DEPTH, 16, 256),
            buf(512, 512),
            buf(256, 1024),
            buf(512, 256),
            buf(512, 256),
            buf(SLOTS, 128, ROWS),
            buf(SLOTS, ROWS, 256),
            buf(SLOTS, 128, ROWS),
            buf(SLOTS, 128, ROWS),
            buf(SLOTS, ROWS, 256),
            buf(2, 128, dtype=F32),
            buf(PLANE, 16, ROWS),
            buf(PLANE, 32, 256),
            buf(PLANE, 16, ROWS),
            buf(PLANE, 16, ROWS),
            buf(PLANE, 32, 256),
            buf(PLANE, 2, 128, dtype=F32),
            buf(16, ROWS),
            buf(8, 32, 256),
            buf(128, 64, dtype=F32),
            pltpu.SemaphoreType.DMA((17,)),
            pltpu.SemaphoreType.DMA((17,)),
            pltpu.SemaphoreType.DMA((7,)),
        ],
        compiler_params=pltpu.CompilerParams(
            collective_id=0, has_side_effects=True, vmem_limit_bytes=40 * 1024 * 1024
        ),
        cost_estimate=pl.CostEstimate(
            flops=2 * 256 * 256 * 4096, bytes_accessed=4 * 1024 * 1024, transcendentals=65536
        ),
    )(
        byte_states,
        shorten_weight.reshape(4, 2, DEPTH, 2, 8, 128),
        norm_gain.reshape(1, 128),
        qkv_weight.reshape(2, DEPTH, 2, 16, 384),
        qk_gain,
        out_weight.reshape(2, DEPTH, 2, 16, 128),
        up_weight.reshape(2, DEPTH, 2, 16, 256),
        doc_lengths,
    )


def solution(mesh):
    placed = (
        P("mp", "ctx"),
        P(None, None, "mp", None, "ctx"),
        P("ctx"),
        P(None, "mp", None, None, "ctx"),
        P(),
        P(None, "mp", None, "ctx"),
        P(None, "mp", None, None, "ctx"),
        P(),
    )
    return jax.shard_map(
        per_device, mesh=mesh, in_specs=placed, out_specs=P("mp", "ctx"), check_vma=False
    )
```

```python
import jax
import jax.numpy as jnp
from jax import lax
from jax.experimental import pallas as pl
from jax.experimental.pallas import tpu as pltpu
from jax.sharding import PartitionSpec as P

F32 = jnp.float32
BF16 = jnp.bfloat16
MESH = pl.DeviceIdType.MESH
ROWS = 256
PLANE = 32
DEPTH = 16
SLOTS = 4


def dot00(a, b):
    return lax.dot_general(a, b, (((0,), (0,)), ((), ())), preferred_element_type=F32)


def kernel(
    bytes_hbm, wconv_hbm, gain_hbm, wqkv_hbm, qk_gain_hbm, wout_hbm, wup_hbm, docs_hbm,
    out_ref,
    bytes_ref, gain_ref, qk_gain_ref, docs_ref,
    p0_wide, p0_send, p0_recv,
    x1, x2, x3, x4,
    gains, gain_own,
    wconv_in, wqkv_in, wout_in, wup_in,
    wconv_t, wqk, wv_t, wout_t,
    s_conv, s_qk, s_v, s_out, s_up, s_sq,
    r_conv, r_qk, r_v, r_out, r_up, r_sq,
    short_own, qk_all,
    send_sem, recv_sem, local_sem,
):
    ctx = lax.axis_index("ctx")
    mp = lax.axis_index("mp")
    y_lo, z, core = lax.div(ctx, 32), lax.rem(lax.div(ctx, 2), DEPTH), lax.rem(ctx, 2)
    y, x = lax.div(mp, 4) * 2 + y_lo, lax.rem(mp, 4)
    slot = y_lo * 2 + core
    me = mp * SLOTS + slot

    def plane_peer(i):
        def offset(k):
            return jnp.where(k == 3, 0, jnp.where(k == 2, 3, 2 - k))

        px = lax.rem(x + offset(lax.div(i, 8)), 4)
        py = lax.rem(y + offset(lax.rem(lax.div(i, 2), 4)), 4)
        pc = lax.rem(core + 1 + lax.rem(i, 2), 2)
        p_lo = lax.rem(py, 2)
        return (p_lo * 32 + z * 2 + pc, lax.div(py, 2) * 4 + px), p_lo * 2 + pc

    def depth_peer(i):
        far = 8 - lax.div(i + 1, 2)
        step = jnp.where(lax.rem(i, 2) == 1, far, DEPTH - far)
        pz = lax.rem(z + step, DEPTH)
        return (y_lo * 32 + pz * 2 + core, mp)

    def loop(count, body):
        def step(i, carry):
            body(i)
            return carry

        lax.fori_loop(0, count, step, 0)

    def put(src, dst, sem, device):
        pltpu.make_async_remote_copy(
            src_ref=src, dst_ref=dst, send_sem=send_sem.at[sem], recv_sem=recv_sem.at[sem],
            device_id=device, device_id_type=MESH,
        ).start()

    def arrived(view, sem):
        pltpu.make_async_copy(view, view, recv_sem.at[sem]).wait()

    def left(view, sem):
        pltpu.make_async_copy(view, view, send_sem.at[sem]).wait()

    def along_depth(buf, sem):
        loop(DEPTH - 1, lambda i: put(buf.at[z], buf.at[z], sem, depth_peer(i)))

    def to_plane(piece, dst, sem):
        def body(i):
            device, its_slot = plane_peer(i)
            put(piece(its_slot, device[1]), dst.at[me], sem, device)

        loop(PLANE - 1, body)

    small = []
    for i, (src, dst) in enumerate(
        ((bytes_hbm, bytes_ref), (gain_hbm, gain_ref), (qk_gain_hbm, qk_gain_ref), (docs_hbm, docs_ref))
    ):
        small.append(pltpu.make_async_copy(src, dst, local_sem.at[7 + i]))
    for copy in small:
        copy.start()

    def near(i):
        far = 4 - lax.div(i, 2)
        return shifted(jnp.where(lax.rem(i, 2) == 0, far, DEPTH - far))

    def shifted(step):
        return lax.rem(z + step, DEPTH)

    def at_depth(pz):
        return (y_lo * 32 + pz * 2 + core, mp)

    def same_slot(i):
        return lax.rem(mp + 1 + i, 8)

    def regroup_peer(i):
        p_lo = lax.rem(y_lo + lax.div(i + 1, 2), 2)
        p_core = lax.rem(core + i + 1, 2)
        return p_lo, p_core, (p_lo * 32 + z * 2 + p_core, mp)

    barrier = pltpu.get_barrier_semaphore()

    def greet(device):
        pl.semaphore_signal(barrier, inc=1, device_id=device, device_id_type=MESH)

    loop(8, lambda i: greet(at_depth(near(i))))
    loop(7, lambda i: greet((ctx, same_slot(i))))
    loop(3, lambda i: greet(regroup_peer(i)[2]))

    own = []
    for tap in range(4):
        own.append((wconv_hbm.at[tap, y_lo, :, core], wconv_in.at[slot, :, tap]))
    for src, dst in ((wqkv_hbm, wqkv_in), (wout_hbm, wout_in), (wup_hbm, wup_in)):
        own.append((src.at[y_lo, :, core], dst.at[slot]))
    own = [pltpu.make_async_copy(a, b, local_sem.at[i]) for i, (a, b) in enumerate(own)]
    for copy in own:
        copy.start()

    for copy in small:
        copy.wait()
    local = bytes_ref[...]
    row = lax.broadcasted_iota(jnp.int32, (128, ROWS), 0)
    col = lax.broadcasted_iota(jnp.int32, (128, ROWS), 1)
    for tap in range(4):
        pick = (row + mp * 128 == 4 * col + (tap - 3)).astype(F32).astype(BF16)
        placed = jnp.dot(local, pick, preferred_element_type=F32)
        for m in range(8):
            p0_wide[m, tap * 8 : tap * 8 + 8, :] = placed[m * 8 : m * 8 + 8, :]
    p0_send[...] = p0_wide[...].astype(BF16)
    p0_recv[mp] = p0_send[mp]

    lane = lax.broadcasted_iota(jnp.int32, (16, 128), 1)
    feat = lax.broadcasted_iota(jnp.int32, (16, 128), 0)
    mine = jnp.where(lane == feat + mp * 16, gain_ref[...], 0.0)
    gain_own[...] = jnp.broadcast_to(jnp.sum(mine, axis=1, keepdims=True), (16, 128))
    gains[z] = gain_own[...]

    pl.semaphore_wait(barrier, 18)

    def trade(i):
        other = same_slot(i)
        put(p0_send.at[other], p0_recv.at[mp], 0, (ctx, other))

    loop(7, trade)

    peers = [regroup_peer(jnp.int32(i)) for i in range(3)]
    for p_lo, p_core, device in peers:
        for tap in range(4):
            put(wconv_hbm.at[tap, p_lo, :, p_core], wconv_in.at[slot, :, tap], 1, device)
    for src, dst, sem in ((wqkv_hbm, wqkv_in, 2), (wout_hbm, wout_in, 3), (wup_hbm, wup_in, 4)):
        for p_lo, p_core, device in peers:
            put(src.at[p_lo, :, p_core], dst.at[slot], sem, device)

    arrived(p0_recv.at[pl.ds(0, 7)], 0)
    block = p0_recv[0].astype(F32)
    for m in range(1, 8):
        block = block + p0_recv[m].astype(F32)
    x1[z] = block.astype(BF16)

    def spread(block, device, sem):
        put(x1.at[block], x1.at[block], sem, at_depth(device))

    ahead, behind = shifted(4), shifted(DEPTH - 4)
    spread(z, ahead, 5)
    spread(z, behind, 17)
    loop(6, lambda i: spread(z, near(i + 2), 18))
    arrived(x1.at[behind], 5)
    loop(4, lambda i: spread(behind, shifted(4 - i), 19))
    arrived(x1.at[ahead], 17)
    loop(3, lambda i: spread(ahead, shifted(DEPTH - 3 + i), 19))

    for copy in own[:4]:
        copy.wait()
    arrived(wconv_in.at[pl.ds(0, 3)], 1)
    for s in range(SLOTS):
        flat = wconv_in[s].astype(F32).reshape(DEPTH * 32, 128)
        wconv_t[s * 128 : s * 128 + 128, :] = flat.T.astype(BF16)

    arrived(x1.at[pl.ds(0, 6)], 18)
    arrived(x1.at[pl.ds(0, 7)], 19)
    loop(DEPTH - 1, lambda i: put(gain_own, gains.at[z], 6, depth_peer(i)))
    conv = jnp.dot(
        wconv_t[...], x1[...].reshape(DEPTH * 32, ROWS), preferred_element_type=F32
    )
    s_conv[...] = conv.astype(BF16).reshape(SLOTS, 128, ROWS)

    def feature_piece(buf):
        return lambda its_slot, m: buf.at[its_slot, pl.ds(pl.multiple_of(m * 16, 16), 16), :]

    def row_piece(buf):
        return lambda its_slot, m: buf.at[its_slot, pl.ds(pl.multiple_of(m * 32, 32), 32), :]

    to_plane(feature_piece(s_conv), r_conv, 7)
    r_conv[me] = s_conv[slot, pl.ds(pl.multiple_of(mp * 16, 16), 16), :]

    def total(buf):
        acc = buf[0].astype(F32)
        for i in range(1, PLANE):
            acc = acc + buf[i].astype(F32)
        return acc

    arrived(r_conv.at[pl.ds(0, 31)], 7)
    short = total(r_conv).astype(BF16)
    short_own[...] = short
    x2[z] = short
    along_depth(x2, 8)

    own[4].wait()
    arrived(wqkv_in.at[pl.ds(0, 3)], 2)
    arrived(gains.at[pl.ds(0, 15)], 6)
    column = gains[...].reshape(256, 128)
    for s in range(SLOTS):
        for kind in range(2):
            wqk[:, s * 256 + kind * 128 : s * 256 + kind * 128 + 128] = (
                wqkv_in[s, :, kind].reshape(256, 128).astype(F32) * column
            ).astype(BF16)
        wv_t[s * 128 : s * 128 + 128, :] = (wqkv_in[s, :, 2].reshape(256, 128).astype(F32) * column).T.astype(BF16)

    own[5].wait()
    arrived(wout_in.at[pl.ds(0, 3)], 3)
    for s in range(SLOTS):
        wout_t[s * 128 : s * 128 + 128, :] = wout_in[s].reshape(256, 128).astype(F32).T.astype(BF16)

    arrived(x2.at[pl.ds(0, 15)], 8)
    gathered = x2[...].reshape(256, ROWS)
    wide = gathered.astype(F32)
    squares = jnp.sum(wide * wide, axis=0, keepdims=True)
    s_sq[0:1, :] = squares[:, :128]
    s_sq[1:2, :] = squares[:, 128:]
    r_sq[me] = s_sq[...]
    qk = dot00(gathered, wqk[...])
    for s in range(SLOTS):
        s_qk[s] = qk[:, s * 256 : s * 256 + 256].astype(BF16)
    to_plane(row_piece(s_qk), r_qk, 9)
    to_plane(lambda its_slot, m: s_sq, r_sq, 10)
    v = jnp.dot(wv_t[...], gathered, preferred_element_type=F32)
    s_v[...] = v.astype(BF16).reshape(SLOTS, 128, ROWS)
    to_plane(feature_piece(s_v), r_v, 11)
    r_qk[me] = s_qk[slot, pl.ds(pl.multiple_of(mp * 32, 32), 32), :]
    r_v[me] = s_v[slot, pl.ds(pl.multiple_of(mp * 16, 16), 16), :]

    key = lax.broadcasted_iota(jnp.int32, (ROWS, ROWS), 0)
    query = lax.broadcasted_iota(jnp.int32, (ROWS, ROWS), 1)
    key_pos = lax.broadcasted_iota(jnp.int32, (ROWS, 1), 0) * 4
    query_pos = lax.broadcasted_iota(jnp.int32, (1, ROWS), 1) * 4
    key_seg = jnp.zeros((ROWS, 1), jnp.int32)
    query_seg = jnp.zeros((1, ROWS), jnp.int32)
    end = jnp.int32(0)
    for d in range(docs_ref.shape[0]):
        end = end + docs_ref[d]
        key_seg = key_seg + (key_pos >= end).astype(jnp.int32)
        query_seg = query_seg + (query_pos >= end).astype(jnp.int32)
    allowed = (key <= query) & (key_seg == query_seg)

    arrived(r_sq.at[pl.ds(0, 31)], 10)
    mean = jnp.sum(r_sq[...], axis=0) / 8192.0
    inverse = lax.rsqrt(mean + 1e-06)
    inverse = jnp.concatenate([inverse[0:1, :], inverse[1:2, :]], axis=1)
    at_row = lax.broadcasted_iota(jnp.int32, (32, ROWS), 0) + mp * 32
    at_lane = lax.broadcasted_iota(jnp.int32, (32, ROWS), 1)
    row_inverse = jnp.sum(jnp.where(at_row == at_lane, inverse, 0.0), axis=1, keepdims=True)

    arrived(r_qk.at[pl.ds(0, 31)], 9)
    both = total(r_qk) * row_inverse
    for kind in range(2):
        part = both[:, kind * 128 : kind * 128 + 128]
        scale = lax.rsqrt(jnp.mean(part * part, axis=1, keepdims=True) + 1e-06)
        qk_all[mp, :, kind * 128 : kind * 128 + 128] = (
            part * scale * qk_gain_ref[kind : kind + 1, :]
        ).astype(BF16)

    def share(i):
        other = same_slot(i)
        put(qk_all.at[mp], qk_all.at[mp], 12, (ctx, other))

    loop(7, share)

    arrived(r_v.at[pl.ds(0, 31)], 11)
    values = (total(r_v) * inverse).astype(BF16)

    arrived(qk_all.at[pl.ds(0, 7)], 12)
    queries = qk_all[:, :, 0:128].reshape(ROWS, 128)
    keys = qk_all[:, :, 128:256].reshape(ROWS, 128)
    scores = lax.dot_general(
        keys, queries, (((1,), (1,)), ((), ())), preferred_element_type=F32
    ) * (1.0 / 128**0.5)
    weights = jnp.where(allowed, jnp.exp(scores), 0.0)
    denominator = jnp.sum(weights, axis=0, keepdims=True)
    numerator = jnp.dot(values, weights.astype(BF16), preferred_element_type=F32)
    x3[z] = (numerator / denominator).astype(BF16)
    along_depth(x3, 13)

    own[6].wait()
    arrived(wup_in.at[pl.ds(0, 3)], 4)

    arrived(x3.at[pl.ds(0, 15)], 13)
    mixed = jnp.dot(wout_t[...], x3[...].reshape(256, ROWS), preferred_element_type=F32)
    s_out[...] = mixed.astype(BF16).reshape(SLOTS, 128, ROWS)
    to_plane(feature_piece(s_out), r_out, 14)
    r_out[me] = s_out[slot, pl.ds(pl.multiple_of(mp * 16, 16), 16), :]
    arrived(r_out.at[pl.ds(0, 31)], 14)
    x4[z] = (short_own[...].astype(F32) + total(r_out)).astype(BF16)
    along_depth(x4, 15)
    arrived(x4.at[pl.ds(0, 15)], 15)
    hidden = x4[...].reshape(256, ROWS)
    for s in range(SLOTS):
        s_up[s] = dot00(hidden, wup_in[s].reshape(256, 256)).astype(BF16)
    to_plane(row_piece(s_up), r_up, 16)
    r_up[me] = s_up[slot, pl.ds(pl.multiple_of(mp * 32, 32), 32), :]

    left(p0_recv.at[pl.ds(0, 7)], 0)
    left(wconv_in.at[pl.ds(0, 3)], 1)
    left(wqkv_in.at[pl.ds(0, 3)], 2)
    left(wout_in.at[pl.ds(0, 3)], 3)
    left(wup_in.at[pl.ds(0, 3)], 4)
    left(x1.at[0], 5)
    left(x1.at[0], 17)
    left(x1.at[pl.ds(0, 6)], 18)
    left(x1.at[pl.ds(0, 7)], 19)
    left(gains.at[pl.ds(0, 15)], 6)
    left(r_conv.at[pl.ds(0, 31)], 7)
    left(x2.at[pl.ds(0, 15)], 8)
    left(r_qk.at[pl.ds(0, 31)], 9)
    left(r_sq.at[pl.ds(0, 31)], 10)
    left(r_v.at[pl.ds(0, 31)], 11)
    left(qk_all.at[pl.ds(0, 7)], 12)
    left(x3.at[pl.ds(0, 15)], 13)
    left(r_out.at[pl.ds(0, 31)], 14)
    left(x4.at[pl.ds(0, 15)], 15)

    arrived(r_up.at[pl.ds(0, 31)], 16)
    upward = total(r_up)
    stacked = jnp.concatenate([upward[:, tap * 64 : tap * 64 + 64] for tap in range(4)], axis=0)
    high = stacked.astype(BF16)
    low = (stacked - high.astype(F32)).astype(BF16)
    row = lax.broadcasted_iota(jnp.int32, (128, 128), 0)
    col = lax.broadcasted_iota(jnp.int32, (128, 128), 1)
    place = (col == 4 * lax.rem(row, 32) + lax.div(row, 32)).astype(F32).astype(BF16)
    out_ref[...] = (bytes_ref[...].astype(F32) + (dot00(high, place) + dot00(low, place))).astype(BF16)
    left(r_up.at[pl.ds(0, 31)], 16)


def per_device(
    byte_states, shorten_weight, norm_gain, qkv_weight, qk_gain, out_weight, up_weight, doc_lengths
):
    vmem = pl.BlockSpec(memory_space=pltpu.VMEM)
    hbm = pl.BlockSpec(memory_space=pl.ANY)

    def buf(*shape, dtype=BF16):
        return pltpu.VMEM(shape, dtype)

    return pl.pallas_call(
        kernel,
        out_shape=jax.ShapeDtypeStruct(byte_states.shape[::-1], BF16),
        in_specs=[hbm] * 8,
        out_specs=vmem,
        scratch_shapes=[
            buf(64, 128),
            buf(1, 128, dtype=F32),
            buf(2, 128, dtype=F32),
            pltpu.SMEM((6,), jnp.int32),
            buf(8, 32, ROWS, dtype=F32),
            buf(8, 32, ROWS),
            buf(8, 32, ROWS),
            buf(DEPTH, 32, ROWS),
            buf(DEPTH, 16, ROWS),
            buf(DEPTH, 16, ROWS),
            buf(DEPTH, 16, ROWS),
            buf(DEPTH, 16, 128, dtype=F32),
            buf(16, 128, dtype=F32),
            buf(SLOTS, DEPTH, 4, 8, 128),
            buf(SLOTS, DEPTH, 3, 16, 128),
            buf(SLOTS, DEPTH, 16, 128),
            buf(SLOTS, DEPTH, 16, 256),
            buf(512, 512),
            buf(256, 1024),
            buf(512, 256),
            buf(512, 256),
            buf(SLOTS, 128, ROWS),
            buf(SLOTS, ROWS, 256),
            buf(SLOTS, 128, ROWS),
            buf(SLOTS, 128, ROWS),
            buf(SLOTS, ROWS, 256),
            buf(2, 128, dtype=F32),
            buf(PLANE, 16, ROWS),
            buf(PLANE, 32, 256),
            buf(PLANE, 16, ROWS),
            buf(PLANE, 16, ROWS),
            buf(PLANE, 32, 256),
            buf(PLANE, 2, 128, dtype=F32),
            buf(16, ROWS),
            buf(8, 32, 256),
            pltpu.SemaphoreType.DMA((20,)),
            pltpu.SemaphoreType.DMA((20,)),
            pltpu.SemaphoreType.DMA((11,)),
        ],
        compiler_params=pltpu.CompilerParams(
            collective_id=0, has_side_effects=True, vmem_limit_bytes=60 * 1024 * 1024
        ),
        cost_estimate=pl.CostEstimate(
            flops=2 * 256 * 256 * 4096, bytes_accessed=4 * 1024 * 1024, transcendentals=65536
        ),
    )(
        byte_states.T,
        shorten_weight.reshape(4, 2, DEPTH, 2, 8, 128),
        norm_gain.reshape(1, 128),
        qkv_weight.transpose(0, 1, 3, 2, 4).reshape(2, DEPTH, 2, 3, 16, 128),
        qk_gain,
        out_weight.reshape(2, DEPTH, 2, 16, 128),
        up_weight.reshape(2, DEPTH, 2, 16, 256),
        doc_lengths,
    ).T


def solution(mesh):
    placed = (
        P("mp", "ctx"),
        P(None, None, "mp", None, "ctx"),
        P("ctx"),
        P(None, "mp", None, None, "ctx"),
        P(),
        P(None, "mp", None, "ctx"),
        P(None, "mp", None, None, "ctx"),
        P(),
    )
    return jax.shard_map(
        per_device, mesh=mesh, in_specs=placed, out_specs=P("mp", "ctx"), check_vma=False
    )
```

```python
import jax
import jax.numpy as jnp
from jax import lax
from jax.experimental import pallas as pl
from jax.experimental.pallas import tpu as pltpu
from jax.sharding import PartitionSpec as P

F32 = jnp.float32
BF16 = jnp.bfloat16
MESH = pl.DeviceIdType.MESH
ROWS = 256
PLANE = 32
DEPTH = 16
SLOTS = 4


def dot00(a, b):
    return lax.dot_general(a, b, (((0,), (0,)), ((), ())), preferred_element_type=F32)


def kernel(
    bytes_hbm, wconv_hbm, gain_hbm, wqkv_hbm, qk_gain_hbm, wout_hbm, wup_hbm, docs_hbm,
    out_ref,
    bytes_ref, gain_ref, qk_gain_ref, docs_ref,
    p0_wide, p0_send, p0_recv,
    x1, x2, x3, x4,
    gains, gain_own,
    wconv_in, wqkv_in, wout_in, wup_in, wup_raw, wup_own,
    wconv_t, wqk, wv_t, wout_t,
    s_conv, s_qk, s_v, s_out, s_up, s_sq,
    r_conv, r_qk, r_v, r_out, r_up, r_sq,
    short_own, qk_all,
    send_sem, recv_sem, local_sem,
):
    ctx = lax.axis_index("ctx")
    mp = lax.axis_index("mp")
    y_lo, z, core = lax.div(ctx, 32), lax.rem(lax.div(ctx, 2), DEPTH), lax.rem(ctx, 2)
    y, x = lax.div(mp, 4) * 2 + y_lo, lax.rem(mp, 4)
    slot = y_lo * 2 + core
    me = mp * SLOTS + slot
    me_half = mp * 2 + y_lo

    def plane_peer(i):
        def offset(k):
            return jnp.where(k == 3, 0, jnp.where(k == 2, 3, 2 - k))

        px = lax.rem(x + offset(lax.div(i, 8)), 4)
        py = lax.rem(y + offset(lax.rem(lax.div(i, 2), 4)), 4)
        pc = lax.rem(core + 1 + lax.rem(i, 2), 2)
        p_lo = lax.rem(py, 2)
        return (p_lo * 32 + z * 2 + pc, lax.div(py, 2) * 4 + px), p_lo * 2 + pc

    def depth_peer(i):
        far = 8 - lax.div(i + 1, 2)
        step = jnp.where(lax.rem(i, 2) == 1, far, DEPTH - far)
        pz = lax.rem(z + step, DEPTH)
        return (y_lo * 32 + pz * 2 + core, mp)

    def loop(count, body):
        def step(i, carry):
            body(i)
            return carry

        lax.fori_loop(0, count, step, 0)

    def put(src, dst, sem, device):
        pltpu.make_async_remote_copy(
            src_ref=src, dst_ref=dst, send_sem=send_sem.at[sem], recv_sem=recv_sem.at[sem],
            device_id=device, device_id_type=MESH,
        ).start()

    def arrived(view, sem):
        pltpu.make_async_copy(view, view, recv_sem.at[sem]).wait()

    def left(view, sem):
        pltpu.make_async_copy(view, view, send_sem.at[sem]).wait()

    def along_depth(buf, sem):
        loop(DEPTH - 1, lambda i: put(buf.at[z], buf.at[z], sem, depth_peer(i)))

    def to_plane(piece, dst, sem):
        def body(i):
            device, its_slot = plane_peer(i)
            put(piece(its_slot, device[1]), dst.at[me], sem, device)

        loop(PLANE - 1, body)

    small = []
    for i, (src, dst) in enumerate(
        ((bytes_hbm, bytes_ref), (gain_hbm, gain_ref), (qk_gain_hbm, qk_gain_ref), (docs_hbm, docs_ref))
    ):
        small.append(pltpu.make_async_copy(src, dst, local_sem.at[7 + i]))
    for copy in small:
        copy.start()

    def near(i):
        far = 4 - lax.div(i, 2)
        return shifted(jnp.where(lax.rem(i, 2) == 0, far, DEPTH - far))

    def shifted(step):
        return lax.rem(z + step, DEPTH)

    def at_depth(pz):
        return (y_lo * 32 + pz * 2 + core, mp)

    def same_slot(i):
        return lax.rem(mp + 1 + i, 8)

    def regroup_peer(i):
        p_lo = lax.rem(y_lo + lax.div(i + 1, 2), 2)
        p_core = lax.rem(core + i + 1, 2)
        return p_lo, p_core, (p_lo * 32 + z * 2 + p_core, mp)

    def to_half(piece, dst, sem):
        def body(i):
            device, its_slot = plane_peer(2 * i + 1)
            put(piece(lax.div(its_slot, 2), device[1]), dst.at[me_half], sem, device)

        loop(PLANE // 2 - 1, body)

    barrier = pltpu.get_barrier_semaphore()

    def greet(device):
        pl.semaphore_signal(barrier, inc=1, device_id=device, device_id_type=MESH)

    loop(8, lambda i: greet(at_depth(near(i))))
    loop(7, lambda i: greet((ctx, same_slot(i))))
    loop(3, lambda i: greet(regroup_peer(i)[2]))

    own = []
    for tap in range(4):
        own.append((wconv_hbm.at[tap, y_lo, :, core], wconv_in.at[slot, :, tap]))
    own.append((wqkv_hbm.at[y_lo], wqkv_in.at[y_lo]))
    own.append((wout_hbm.at[y_lo, :, core], wout_in.at[slot]))
    own = [pltpu.make_async_copy(a, b, local_sem.at[i]) for i, (a, b) in enumerate(own)]
    for copy in own:
        copy.start()
    raw_up = pltpu.make_async_copy(wup_hbm, wup_raw, local_sem.at[6])
    raw_up.start()

    for copy in small:
        copy.wait()
    local = bytes_ref[...]
    row = lax.broadcasted_iota(jnp.int32, (128, ROWS), 0)
    col = lax.broadcasted_iota(jnp.int32, (128, ROWS), 1)
    for tap in range(4):
        pick = (row + mp * 128 == 4 * col + (tap - 3)).astype(F32).astype(BF16)
        placed = jnp.dot(local, pick, preferred_element_type=F32)
        for m in range(8):
            p0_wide[m, tap * 8 : tap * 8 + 8, :] = placed[m * 8 : m * 8 + 8, :]
    p0_send[...] = p0_wide[...].astype(BF16)
    p0_recv[mp] = p0_send[mp]

    lane = lax.broadcasted_iota(jnp.int32, (16, 128), 1)
    feat = lax.broadcasted_iota(jnp.int32, (16, 128), 0)
    mine = jnp.where(lane == feat + mp * 16, gain_ref[...], 0.0)
    gain_own[...] = jnp.broadcast_to(jnp.sum(mine, axis=1, keepdims=True), (16, 128))
    gains[z, core] = gain_own[...]

    raw_up.wait()
    row = lax.broadcasted_iota(jnp.int32, (256, 256), 0)
    col = lax.broadcasted_iota(jnp.int32, (256, 256), 1)
    sort = (col == 4 * lax.rem(row, 64) + lax.div(row, 64)).astype(F32).astype(BF16)
    for lo in range(2):
        for quarter in range(8):
            rows = wup_raw[lo, quarter * 2 : quarter * 2 + 2].reshape(256, 64)
            taps = jnp.dot(sort, rows, preferred_element_type=F32).astype(BF16)
            wup_own[lo, quarter * 2 : quarter * 2 + 2] = jnp.concatenate(
                [taps[tap * 64 : tap * 64 + 64] for tap in range(4)], axis=1
            ).reshape(2, 2, 16, 256)
    wup_in[y_lo] = wup_own[y_lo]

    pl.semaphore_wait(barrier, 18)

    def trade(i):
        other = same_slot(i)
        put(p0_send.at[other], p0_recv.at[mp], 0, (ctx, other))

    loop(7, trade)

    across = ((1 - y_lo) * 32 + z * 2 + core, mp)
    twin = (ctx + 1 - 2 * core, mp)
    peers = [regroup_peer(jnp.int32(i)) for i in range(3)]
    for p_lo, p_core, device in peers:
        for tap in range(4):
            put(wconv_hbm.at[tap, p_lo, :, p_core], wconv_in.at[slot, :, tap], 1, device)
    arrived(p0_recv.at[pl.ds(0, 7)], 0)
    block = p0_recv[0].astype(F32)
    for m in range(1, 8):
        block = block + p0_recv[m].astype(F32)
    x1[z] = block.astype(BF16)

    def spread(block, device, sem):
        put(x1.at[block], x1.at[block], sem, at_depth(device))

    ahead, behind = shifted(4), shifted(DEPTH - 4)
    spread(z, ahead, 5)
    spread(z, behind, 17)
    loop(6, lambda i: spread(z, near(i + 2), 18))
    put(wqkv_hbm.at[1 - y_lo], wqkv_in.at[y_lo], 2, across)
    arrived(x1.at[behind], 5)
    loop(4, lambda i: spread(behind, shifted(4 - i), 19))
    arrived(x1.at[ahead], 17)
    loop(3, lambda i: spread(ahead, shifted(DEPTH - 3 + i), 19))

    for copy in own[:4]:
        copy.wait()
    arrived(wconv_in.at[pl.ds(0, 3)], 1)
    for s in range(SLOTS):
        flat = wconv_in[s].astype(F32).reshape(DEPTH * 32, 128)
        wconv_t[s * 128 : s * 128 + 128, :] = flat.T.astype(BF16)

    arrived(x1.at[pl.ds(0, 6)], 18)
    arrived(x1.at[pl.ds(0, 7)], 19)
    conv = jnp.dot(
        wconv_t[...], x1[...].reshape(DEPTH * 32, ROWS), preferred_element_type=F32
    )
    s_conv[...] = conv.astype(BF16).reshape(SLOTS, 128, ROWS)

    def feature_piece(buf):
        return lambda its_slot, m: buf.at[its_slot, pl.ds(pl.multiple_of(m * 16, 16), 16), :]

    def row_piece(buf):
        return lambda its_slot, m: buf.at[its_slot, pl.ds(pl.multiple_of(m * 32, 32), 32), :]

    to_plane(feature_piece(s_conv), r_conv, 7)
    loop(DEPTH - 1, lambda i: put(gain_own, gains.at[z, core], 6, depth_peer(i)))
    r_conv[me] = s_conv[slot, pl.ds(pl.multiple_of(mp * 16, 16), 16), :]

    def total(buf):
        acc = buf[0].astype(F32)
        for i in range(1, buf.shape[0]):
            acc = acc + buf[i].astype(F32)
        return acc

    arrived(r_conv.at[pl.ds(0, 31)], 7)
    short = total(r_conv).astype(BF16)
    short_own[...] = short
    x2[z, core] = short
    along_depth(x2.at[:, core], 8)
    for p_lo, p_core, device in peers:
        put(wout_hbm.at[p_lo, :, p_core], wout_in.at[slot], 3, device)

    own[4].wait()
    arrived(wqkv_in.at[0], 2)
    arrived(gains.at[pl.ds(0, 15), 0], 6)
    put(gains.at[:, core], gains.at[:, core], 20, twin)
    arrived(gains.at[:, 0], 20)
    column = gains[...].reshape(512, 128)
    for s in range(2):
        for kind in range(2):
            wqk[:, s * 256 + kind * 128 : s * 256 + kind * 128 + 128] = (
                wqkv_in[s, :, :, kind].reshape(512, 128).astype(F32) * column
            ).astype(BF16)
        wv_t[s * 128 : s * 128 + 128, :] = (
            (wqkv_in[s, :, :, 2].reshape(512, 128).astype(F32) * column).T.astype(BF16)
        )

    arrived(x2.at[pl.ds(0, 15), 0], 8)
    put(x2.at[:, core], x2.at[:, core], 21, twin)
    arrived(x2.at[:, 0], 21)
    gathered = x2[...].reshape(512, ROWS)
    wide = gathered.astype(F32)
    squares = jnp.sum(wide * wide, axis=0, keepdims=True)
    s_sq[0:1, :] = squares[:, :128]
    s_sq[1:2, :] = squares[:, 128:]
    r_sq[me_half] = s_sq[...]
    qk = dot00(gathered, wqk[...])
    for s in range(2):
        s_qk[s] = qk[:, s * 256 : s * 256 + 256].astype(BF16)
    to_half(row_piece(s_qk), r_qk, 9)
    to_half(lambda its_lo, m: s_sq, r_sq, 10)
    v = jnp.dot(wv_t[...], gathered, preferred_element_type=F32)
    s_v[...] = v.astype(BF16).reshape(2, 128, ROWS)
    to_half(feature_piece(s_v), r_v, 11)
    r_qk[me_half] = s_qk[y_lo, pl.ds(pl.multiple_of(mp * 32, 32), 32), :]
    r_v[me_half] = s_v[y_lo, pl.ds(pl.multiple_of(mp * 16, 16), 16), :]

    own[5].wait()
    arrived(wout_in.at[pl.ds(0, 3)], 3)
    for s in range(SLOTS):
        wout_t[s * 128 : s * 128 + 128, :] = wout_in[s].reshape(256, 128).astype(F32).T.astype(BF16)

    key = lax.broadcasted_iota(jnp.int32, (ROWS, ROWS), 0)
    query = lax.broadcasted_iota(jnp.int32, (ROWS, ROWS), 1)
    key_pos = lax.broadcasted_iota(jnp.int32, (ROWS, 1), 0) * 4
    query_pos = lax.broadcasted_iota(jnp.int32, (1, ROWS), 1) * 4
    key_seg = jnp.zeros((ROWS, 1), jnp.int32)
    query_seg = jnp.zeros((1, ROWS), jnp.int32)
    end = jnp.int32(0)
    for d in range(docs_ref.shape[0]):
        end = end + docs_ref[d]
        key_seg = key_seg + (key_pos >= end).astype(jnp.int32)
        query_seg = query_seg + (query_pos >= end).astype(jnp.int32)
    allowed = (key <= query) & (key_seg == query_seg)

    arrived(r_sq.at[pl.ds(0, 15)], 10)
    mean = jnp.sum(r_sq[...], axis=0) / 8192.0
    inverse = lax.rsqrt(mean + 1e-06)
    inverse = jnp.concatenate([inverse[0:1, :], inverse[1:2, :]], axis=1)
    at_row = lax.broadcasted_iota(jnp.int32, (32, ROWS), 0) + mp * 32
    at_lane = lax.broadcasted_iota(jnp.int32, (32, ROWS), 1)
    row_inverse = jnp.sum(jnp.where(at_row == at_lane, inverse, 0.0), axis=1, keepdims=True)

    arrived(r_qk.at[pl.ds(0, 15)], 9)
    both = total(r_qk) * row_inverse
    for kind in range(2):
        part = both[:, kind * 128 : kind * 128 + 128]
        scale = lax.rsqrt(jnp.mean(part * part, axis=1, keepdims=True) + 1e-06)
        qk_all[mp, :, kind * 128 : kind * 128 + 128] = (
            part * scale * qk_gain_ref[kind : kind + 1, :]
        ).astype(BF16)

    def share(i):
        other = same_slot(i)
        put(qk_all.at[mp], qk_all.at[mp], 12, (ctx, other))

    loop(7, share)

    arrived(r_v.at[pl.ds(0, 15)], 11)
    values = (total(r_v) * inverse).astype(BF16)

    arrived(qk_all.at[pl.ds(0, 7)], 12)
    queries = qk_all[:, :, 0:128].reshape(ROWS, 128)
    keys = qk_all[:, :, 128:256].reshape(ROWS, 128)
    scores = lax.dot_general(
        keys, queries, (((1,), (1,)), ((), ())), preferred_element_type=F32
    ) * (1.0 / 128**0.5)
    weights = jnp.where(allowed, jnp.exp(scores), 0.0)
    denominator = jnp.sum(weights, axis=0, keepdims=True)
    numerator = jnp.dot(values, weights.astype(BF16), preferred_element_type=F32)
    x3[z] = (numerator / denominator).astype(BF16)
    along_depth(x3, 13)
    put(wup_own.at[1 - y_lo], wup_in.at[y_lo], 4, across)

    arrived(wup_in.at[0], 4)

    arrived(x3.at[pl.ds(0, 15)], 13)
    mixed = jnp.dot(wout_t[...], x3[...].reshape(256, ROWS), preferred_element_type=F32)
    s_out[...] = mixed.astype(BF16).reshape(SLOTS, 128, ROWS)
    to_plane(feature_piece(s_out), r_out, 14)
    r_out[me] = s_out[slot, pl.ds(pl.multiple_of(mp * 16, 16), 16), :]
    arrived(r_out.at[pl.ds(0, 31)], 14)
    x4[z, core] = (short_own[...].astype(F32) + total(r_out)).astype(BF16)
    along_depth(x4.at[:, core], 15)
    arrived(x4.at[pl.ds(0, 15), 0], 15)
    put(x4.at[:, core], x4.at[:, core], 22, twin)
    arrived(x4.at[:, 0], 22)
    hidden = x4[...].reshape(512, ROWS)
    for s in range(2):
        s_up[s] = dot00(hidden, wup_in[s].reshape(512, 256)).astype(BF16)
    to_half(row_piece(s_up), r_up, 16)
    r_up[me_half] = s_up[y_lo, pl.ds(pl.multiple_of(mp * 32, 32), 32), :]

    left(p0_recv.at[pl.ds(0, 7)], 0)
    left(wconv_in.at[pl.ds(0, 3)], 1)
    left(wqkv_in.at[0], 2)
    left(wout_in.at[pl.ds(0, 3)], 3)
    left(wup_in.at[0], 4)
    left(x1.at[0], 5)
    left(x1.at[0], 17)
    left(x1.at[pl.ds(0, 6)], 18)
    left(x1.at[pl.ds(0, 7)], 19)
    left(gains.at[pl.ds(0, 15), 0], 6)
    left(gains.at[:, 0], 20)
    left(r_conv.at[pl.ds(0, 31)], 7)
    left(x2.at[pl.ds(0, 15), 0], 8)
    left(x2.at[:, 0], 21)
    left(r_qk.at[pl.ds(0, 15)], 9)
    left(r_sq.at[pl.ds(0, 15)], 10)
    left(r_v.at[pl.ds(0, 15)], 11)
    left(qk_all.at[pl.ds(0, 7)], 12)
    left(x3.at[pl.ds(0, 15)], 13)
    left(r_out.at[pl.ds(0, 31)], 14)
    left(x4.at[pl.ds(0, 15), 0], 15)
    left(x4.at[:, 0], 22)

    arrived(r_up.at[pl.ds(0, 15)], 16)
    upward = total(r_up)
    stacked = jnp.concatenate([upward[:, tap * 64 : tap * 64 + 64] for tap in range(4)], axis=0)
    high = stacked.astype(BF16)
    low = (stacked - high.astype(F32)).astype(BF16)
    row = lax.broadcasted_iota(jnp.int32, (128, 128), 0)
    col = lax.broadcasted_iota(jnp.int32, (128, 128), 1)
    place = (col == 4 * lax.rem(row, 32) + lax.div(row, 32)).astype(F32).astype(BF16)
    out_ref[...] = (bytes_ref[...].astype(F32) + (dot00(high, place) + dot00(low, place))).astype(BF16)
    left(r_up.at[pl.ds(0, 15)], 16)


def per_device(
    byte_states, shorten_weight, norm_gain, qkv_weight, qk_gain, out_weight, up_weight, doc_lengths
):
    vmem = pl.BlockSpec(memory_space=pltpu.VMEM)
    hbm = pl.BlockSpec(memory_space=pl.ANY)

    def buf(*shape, dtype=BF16):
        return pltpu.VMEM(shape, dtype)

    return pl.pallas_call(
        kernel,
        out_shape=jax.ShapeDtypeStruct(byte_states.shape[::-1], BF16),
        in_specs=[hbm] * 8,
        out_specs=vmem,
        scratch_shapes=[
            buf(64, 128),
            buf(1, 128, dtype=F32),
            buf(2, 128, dtype=F32),
            pltpu.SMEM((6,), jnp.int32),
            buf(8, 32, ROWS, dtype=F32),
            buf(8, 32, ROWS),
            buf(8, 32, ROWS),
            buf(DEPTH, 32, ROWS),
            buf(DEPTH, 2, 16, ROWS),
            buf(DEPTH, 16, ROWS),
            buf(DEPTH, 2, 16, ROWS),
            buf(DEPTH, 2, 16, 128, dtype=F32),
            buf(16, 128, dtype=F32),
            buf(SLOTS, DEPTH, 4, 8, 128),
            buf(2, DEPTH, 2, 3, 16, 128),
            buf(SLOTS, DEPTH, 16, 128),
            buf(2, DEPTH, 2, 16, 256),
            buf(2, DEPTH, 2, 64, 64),
            buf(2, DEPTH, 2, 16, 256),
            buf(512, 512),
            buf(512, 512),
            buf(256, 512),
            buf(512, 256),
            buf(SLOTS, 128, ROWS),
            buf(2, ROWS, 256),
            buf(2, 128, ROWS),
            buf(SLOTS, 128, ROWS),
            buf(2, ROWS, 256),
            buf(2, 128, dtype=F32),
            buf(PLANE, 16, ROWS),
            buf(PLANE // 2, 32, 256),
            buf(PLANE // 2, 16, ROWS),
            buf(PLANE, 16, ROWS),
            buf(PLANE // 2, 32, 256),
            buf(PLANE // 2, 2, 128, dtype=F32),
            buf(16, ROWS),
            buf(8, 32, 256),
            pltpu.SemaphoreType.DMA((23,)),
            pltpu.SemaphoreType.DMA((23,)),
            pltpu.SemaphoreType.DMA((11,)),
        ],
        compiler_params=pltpu.CompilerParams(
            collective_id=0, has_side_effects=True, vmem_limit_bytes=60 * 1024 * 1024
        ),
        cost_estimate=pl.CostEstimate(
            flops=2 * 256 * 256 * 4096, bytes_accessed=4 * 1024 * 1024, transcendentals=65536
        ),
    )(
        byte_states.T,
        shorten_weight.reshape(4, 2, DEPTH, 2, 8, 128),
        norm_gain.reshape(1, 128),
        qkv_weight.transpose(0, 1, 3, 2, 4).reshape(2, DEPTH, 2, 3, 16, 128),
        qk_gain,
        out_weight.reshape(2, DEPTH, 2, 16, 128),
        up_weight.reshape(2, DEPTH, 2, 64, 64),
        doc_lengths,
    ).T


def solution(mesh):
    placed = (
        P("mp", "ctx"),
        P(None, None, "mp", None, "ctx"),
        P("ctx"),
        P(None, "mp", None, None, "ctx"),
        P(),
        P(None, "mp", None, "ctx"),
        P(None, "mp", None, None, "ctx"),
        P(),
    )
    return jax.shard_map(
        per_device, mesh=mesh, in_specs=placed, out_specs=P("mp", "ctx"), check_vma=False
    )
```

```python
import jax
import jax.numpy as jnp
from jax import lax
from jax.experimental import pallas as pl
from jax.experimental.pallas import tpu as pltpu
from jax.sharding import PartitionSpec as P

F32 = jnp.float32
BF16 = jnp.bfloat16
MESH = pl.DeviceIdType.MESH
ROWS = 256
PLANE = 32
DEPTH = 16
SLOTS = 4


def dot00(a, b):
    return lax.dot_general(a, b, (((0,), (0,)), ((), ())), preferred_element_type=F32)


def kernel(
    bytes_hbm, wconv_hbm, gain_hbm, wqkv_hbm, qk_gain_hbm, wout_hbm, wup_hbm, docs_hbm,
    out_ref,
    bytes_ref, gain_ref, qk_gain_ref, docs_ref,
    p0_wide, p0_send, p0_recv,
    x1, x2, x3, x4,
    gains, column,
    wconv_in, wqkv_in, wout_in, wup_in, wup_raw, wup_own,
    wconv_t, wqk, wv_t, wout_t,
    s_conv, s_qk, s_v, s_out, s_up, s_sq,
    r_conv, r_qk, r_v, r_out, r_up, r_sq,
    short_own, qk_all,
    send_sem, recv_sem, local_sem,
):
    ctx = lax.axis_index("ctx")
    mp = lax.axis_index("mp")
    y_lo, z, core = lax.div(ctx, 32), lax.rem(lax.div(ctx, 2), DEPTH), lax.rem(ctx, 2)
    x = lax.rem(mp, 4)
    slot = y_lo * 2 + core
    me = mp * SLOTS + slot
    me_half = mp * 2 + y_lo

    lows = [1 - y_lo, y_lo]
    cores = [1 - core, core]
    columns = [lax.rem(x + step, 4) for step in (2, 1, 3, 0)]
    y_hi = lax.div(mp, 4)
    owners = [h * 4 + c for h in (1 - y_hi, y_hi) for c in columns]

    def depth_peer(i):
        far = 8 - (i + 1) // 2
        pz = lax.rem(z + (far if i % 2 else DEPTH - far), DEPTH)
        return (y_lo * 32 + pz * 2 + core, mp)

    def loop(count, body):
        for i in range(count):
            body(i)

    def put(src, dst, sem, device):
        pltpu.make_async_remote_copy(
            src_ref=src, dst_ref=dst, send_sem=send_sem.at[sem], recv_sem=recv_sem.at[sem],
            device_id=device, device_id_type=MESH,
        ).start()

    def arrived(view, sem):
        pltpu.make_async_copy(view, view, recv_sem.at[sem]).wait()

    def left(view, sem):
        pltpu.make_async_copy(view, view, send_sem.at[sem]).wait()

    def along_depth(buf, sem):
        loop(DEPTH - 1, lambda i: put(buf.at[z], buf.at[z], sem, depth_peer(i)))

    def to_slot(low, c, piece, dst, at, sem, itself):
        for owner in owners[: 7 if itself else 8]:
            put(piece(owner), dst.at[at], sem, (low * 32 + z * 2 + c, owner))

    def feature_sums(weights_t, block, sums, dst, sem):
        for low in lows:
            for c in cores:
                its_slot = low * 2 + c
                rows = pl.ds(pl.multiple_of(its_slot * 128, 128), 128)
                part = jnp.dot(weights_t[rows, :], block, preferred_element_type=F32)
                sums[its_slot] = part.astype(BF16)
                piece = feature_piece(sums, its_slot)
                to_slot(low, c, piece, dst, me, sem, low is y_lo and c is core)
        dst[me] = sums[slot, pl.ds(pl.multiple_of(mp * 16, 16), 16), :]

    def feature_piece(buf, at):
        return lambda m: buf.at[at, pl.ds(pl.multiple_of(m * 16, 16), 16), :]

    def row_piece(buf, at):
        return lambda m: buf.at[at, pl.ds(pl.multiple_of(m * 32, 32), 32), :]

    def to_half(piece, dst, sem):
        for low in lows:
            to_slot(low, core, piece(low), dst, me_half, sem, low is y_lo)

    small = []
    for i, (src, dst) in enumerate(
        ((bytes_hbm, bytes_ref), (gain_hbm, gain_ref), (qk_gain_hbm, qk_gain_ref), (docs_hbm, docs_ref))
    ):
        small.append(pltpu.make_async_copy(src, dst, local_sem.at[7 + i]))
    for copy in small:
        copy.start()

    def near(i):
        far = 4 - i // 2
        return shifted(DEPTH - far if i % 2 else far)

    def shifted(step):
        return lax.rem(z + step, DEPTH)

    def at_depth(pz):
        return (y_lo * 32 + pz * 2 + core, mp)

    def same_slot(i):
        return lax.rem(mp + 1 + i, 8)

    def regroup_peer(i):
        p_lo = lax.rem(y_lo + (i + 1) // 2, 2)
        p_core = lax.rem(core + i + 1, 2)
        return p_lo, p_core, (p_lo * 32 + z * 2 + p_core, mp)

    barrier = pltpu.get_barrier_semaphore()

    def greet(device):
        pl.semaphore_signal(barrier, inc=1, device_id=device, device_id_type=MESH)

    loop(8, lambda i: greet(at_depth(near(i))))
    loop(7, lambda i: greet((ctx, same_slot(i))))
    loop(3, lambda i: greet(regroup_peer(i)[2]))

    own = []
    for tap in range(4):
        own.append((wconv_hbm.at[tap, y_lo, :, core], wconv_in.at[slot, :, tap]))
    own.append((wqkv_hbm.at[y_lo], wqkv_in.at[y_lo]))
    own.append((wout_hbm.at[y_lo, :, core], wout_in.at[slot]))
    own = [pltpu.make_async_copy(a, b, local_sem.at[i]) for i, (a, b) in enumerate(own)]
    for copy in own:
        copy.start()
    raw_up = pltpu.make_async_copy(wup_hbm, wup_raw, local_sem.at[6])
    raw_up.start()

    for copy in small:
        copy.wait()
    local = bytes_ref[...]
    row = lax.broadcasted_iota(jnp.int32, (128, ROWS), 0)
    col = lax.broadcasted_iota(jnp.int32, (128, ROWS), 1)
    for tap in range(4):
        pick = (row + mp * 128 == 4 * col + (tap - 3)).astype(F32).astype(BF16)
        placed = jnp.dot(local, pick, preferred_element_type=F32)
        for m in range(8):
            p0_wide[m, tap * 8 : tap * 8 + 8, :] = placed[m * 8 : m * 8 + 8, :]
    p0_send[...] = p0_wide[...].astype(BF16)
    p0_recv[mp] = p0_send[mp]

    pl.semaphore_wait(barrier, 18)

    def trade(i):
        other = same_slot(i)
        put(p0_send.at[other], p0_recv.at[mp], 0, (ctx, other))

    loop(7, trade)

    across = ((1 - y_lo) * 32 + z * 2 + core, mp)
    twin = (ctx + 1 - 2 * core, mp)
    peers = [regroup_peer(jnp.int32(i)) for i in range(3)]
    for p_lo, p_core, device in peers:
        for tap in range(4):
            put(wconv_hbm.at[tap, p_lo, :, p_core], wconv_in.at[slot, :, tap], 1, device)
    arrived(p0_recv.at[pl.ds(0, 7)], 0)
    block = p0_recv[0].astype(F32)
    for m in range(1, 8):
        block = block + p0_recv[m].astype(F32)
    x1[z] = block.astype(BF16)

    def spread(block, device, sem):
        put(x1.at[block], x1.at[block], sem, at_depth(device))

    ahead, behind = shifted(4), shifted(DEPTH - 4)
    spread(z, ahead, 5)
    spread(z, behind, 17)
    loop(6, lambda i: spread(z, near(i + 2), 18))
    put(wqkv_hbm.at[1 - y_lo], wqkv_in.at[y_lo], 2, across)
    arrived(x1.at[behind], 5)
    loop(4, lambda i: spread(behind, shifted(4 - i), 19))
    arrived(x1.at[ahead], 17)
    loop(3, lambda i: spread(ahead, shifted(DEPTH - 3 + i), 19))

    for copy in own[:4]:
        copy.wait()
    arrived(wconv_in.at[pl.ds(0, 3)], 1)
    for s in range(SLOTS):
        flat = wconv_in[s].astype(F32).reshape(DEPTH * 32, 128)
        wconv_t[s * 128 : s * 128 + 128, :] = flat.T.astype(BF16)

    arrived(x1.at[pl.ds(0, 6)], 18)
    arrived(x1.at[pl.ds(0, 7)], 19)
    feature_sums(wconv_t, x1[...].reshape(DEPTH * 32, ROWS), s_conv, r_conv, 7)
    loop(DEPTH - 1, lambda i: put(gain_ref, gains.at[core, z], 6, depth_peer(i)))

    raw_up.wait()
    row = lax.broadcasted_iota(jnp.int32, (256, 256), 0)
    col = lax.broadcasted_iota(jnp.int32, (256, 256), 1)
    sort = (col == 4 * lax.rem(row, 64) + lax.div(row, 64)).astype(F32).astype(BF16)
    for lo, c, quarter in ((a, b, q) for a in range(2) for b in range(2) for q in range(4)):
        rows = wup_raw[lo, quarter * 4 : quarter * 4 + 4, c].reshape(256, 64)
        taps = jnp.dot(sort, rows, preferred_element_type=F32).astype(BF16)
        wup_own[lo, c, quarter * 4 : quarter * 4 + 4] = jnp.concatenate(
            [taps[tap * 64 : tap * 64 + 64] for tap in range(4)], axis=1
        ).reshape(4, 16, 256)
    wup_in[y_lo] = wup_own[y_lo]

    def total(buf):
        acc = buf[0].astype(F32)
        for i in range(1, buf.shape[0]):
            acc = acc + buf[i].astype(F32)
        return acc

    arrived(r_conv.at[pl.ds(0, 31)], 7)
    short = total(r_conv).astype(BF16)
    short_own[...] = short
    x2[core, z] = short
    along_depth(x2.at[core], 8)
    for p_lo, p_core, device in peers:
        put(wout_hbm.at[p_lo, :, p_core], wout_in.at[slot], 3, device)

    own[4].wait()
    arrived(wqkv_in.at[0], 2)
    arrived(gains.at[0, pl.ds(0, 15)], 6)
    gains[core, z] = gain_ref[...]
    put(gains.at[core], gains.at[core], 20, twin)
    arrived(gains.at[0], 20)
    lane = lax.broadcasted_iota(jnp.int32, (16, 128), 1)
    feat = lax.broadcasted_iota(jnp.int32, (16, 128), 0)
    for c in range(2):
        for d in range(DEPTH):
            mine = jnp.where(lane == feat + mp * 16, gains[c, d], 0.0)
            column[c, d] = jnp.broadcast_to(jnp.sum(mine, axis=1, keepdims=True), (16, 128))
    for c in range(2):
        gain_rows = column[c].reshape(256, 128)
        for s in range(2):
            for kind in range(2):
                w = wqkv_in[s, :, c, kind].reshape(256, 128).astype(F32) * gain_rows
                at = kind * 128
                wqk[s, c * 256 : c * 256 + 256, at : at + 128] = w.astype(BF16)
            w = wqkv_in[s, :, c, 2].reshape(256, 128).astype(F32) * gain_rows
            wv_t[s * 128 : s * 128 + 128, c * 256 : c * 256 + 256] = w.T.astype(BF16)

    arrived(x2.at[0, pl.ds(0, 15)], 8)
    put(x2.at[core], x2.at[core], 21, twin)
    arrived(x2.at[0], 21)
    gathered = x2[...].reshape(512, ROWS)
    for low in lows:
        s_qk[low] = dot00(gathered, wqk[low]).astype(BF16)
        to_slot(low, core, row_piece(s_qk, low), r_qk, me_half, 9, low is y_lo)
    wide = gathered.astype(F32)
    squares = jnp.sum(wide * wide, axis=0, keepdims=True)
    s_sq[0:1, :] = squares[:, :128]
    s_sq[1:2, :] = squares[:, 128:]
    r_sq[me_half] = s_sq[...]
    to_half(lambda low: lambda m: s_sq, r_sq, 10)
    v = jnp.dot(wv_t[...], gathered, preferred_element_type=F32)
    s_v[...] = v.astype(BF16).reshape(2, 128, ROWS)
    to_half(lambda low: feature_piece(s_v, low), r_v, 11)
    r_qk[me_half] = s_qk[y_lo, pl.ds(pl.multiple_of(mp * 32, 32), 32), :]
    r_v[me_half] = s_v[y_lo, pl.ds(pl.multiple_of(mp * 16, 16), 16), :]

    own[5].wait()
    arrived(wout_in.at[pl.ds(0, 3)], 3)
    for s in range(SLOTS):
        wout_t[s * 128 : s * 128 + 128, :] = wout_in[s].reshape(256, 128).astype(F32).T.astype(BF16)

    key = lax.broadcasted_iota(jnp.int32, (ROWS, ROWS), 0)
    query = lax.broadcasted_iota(jnp.int32, (ROWS, ROWS), 1)
    key_pos = lax.broadcasted_iota(jnp.int32, (ROWS, 1), 0) * 4
    query_pos = lax.broadcasted_iota(jnp.int32, (1, ROWS), 1) * 4
    key_seg = jnp.zeros((ROWS, 1), jnp.int32)
    query_seg = jnp.zeros((1, ROWS), jnp.int32)
    end = jnp.int32(0)
    for d in range(docs_ref.shape[0]):
        end = end + docs_ref[d]
        key_seg = key_seg + (key_pos >= end).astype(jnp.int32)
        query_seg = query_seg + (query_pos >= end).astype(jnp.int32)
    allowed = (key <= query) & (key_seg == query_seg)

    arrived(r_sq.at[pl.ds(0, 15)], 10)
    mean = jnp.sum(r_sq[...], axis=0) / 8192.0
    inverse = lax.rsqrt(mean + 1e-06)
    inverse = jnp.concatenate([inverse[0:1, :], inverse[1:2, :]], axis=1)
    at_row = lax.broadcasted_iota(jnp.int32, (32, ROWS), 0) + mp * 32
    at_lane = lax.broadcasted_iota(jnp.int32, (32, ROWS), 1)
    row_inverse = jnp.sum(jnp.where(at_row == at_lane, inverse, 0.0), axis=1, keepdims=True)

    arrived(r_qk.at[pl.ds(0, 15)], 9)
    both = total(r_qk) * row_inverse
    for kind in range(2):
        part = both[:, kind * 128 : kind * 128 + 128]
        scale = lax.rsqrt(jnp.mean(part * part, axis=1, keepdims=True) + 1e-06)
        qk_all[mp, :, kind * 128 : kind * 128 + 128] = (
            part * scale * qk_gain_ref[kind : kind + 1, :]
        ).astype(BF16)

    def share(i):
        other = same_slot(i)
        put(qk_all.at[mp], qk_all.at[mp], 12, (ctx, other))

    loop(7, share)

    arrived(r_v.at[pl.ds(0, 15)], 11)
    values = (total(r_v) * inverse).astype(BF16)

    arrived(qk_all.at[pl.ds(0, 7)], 12)
    queries = qk_all[:, :, 0:128].reshape(ROWS, 128)
    keys = qk_all[:, :, 128:256].reshape(ROWS, 128)
    scores = lax.dot_general(
        keys, queries, (((1,), (1,)), ((), ())), preferred_element_type=F32
    ) * (1.0 / 128**0.5)
    weights = jnp.where(allowed, jnp.exp(scores), 0.0)
    denominator = jnp.sum(weights, axis=0, keepdims=True)
    numerator = jnp.dot(values, weights.astype(BF16), preferred_element_type=F32)
    x3[z] = (numerator / denominator).astype(BF16)
    along_depth(x3, 13)
    put(wup_own.at[1 - y_lo], wup_in.at[y_lo], 4, across)

    arrived(wup_in.at[0], 4)

    arrived(x3.at[pl.ds(0, 15)], 13)
    feature_sums(wout_t, x3[...].reshape(256, ROWS), s_out, r_out, 14)
    arrived(r_out.at[pl.ds(0, 31)], 14)
    x4[core, z] = (short_own[...].astype(F32) + total(r_out)).astype(BF16)
    along_depth(x4.at[core], 15)
    arrived(x4.at[0, pl.ds(0, 15)], 15)
    put(x4.at[core], x4.at[core], 22, twin)
    arrived(x4.at[0], 22)
    hidden = x4[...].reshape(512, ROWS)
    for low in lows:
        s_up[low] = dot00(hidden, wup_in[low].reshape(512, 256)).astype(BF16)
        to_slot(low, core, row_piece(s_up, low), r_up, me_half, 16, low is y_lo)
    r_up[me_half] = s_up[y_lo, pl.ds(pl.multiple_of(mp * 32, 32), 32), :]

    left(p0_recv.at[pl.ds(0, 7)], 0)
    left(wconv_in.at[pl.ds(0, 3)], 1)
    left(wqkv_in.at[0], 2)
    left(wout_in.at[pl.ds(0, 3)], 3)
    left(wup_in.at[0], 4)
    left(x1.at[0], 5)
    left(x1.at[0], 17)
    left(x1.at[pl.ds(0, 6)], 18)
    left(x1.at[pl.ds(0, 7)], 19)
    left(gains.at[0, pl.ds(0, 15)], 6)
    left(gains.at[0], 20)
    left(r_conv.at[pl.ds(0, 31)], 7)
    left(x2.at[0, pl.ds(0, 15)], 8)
    left(x2.at[0], 21)
    left(r_qk.at[pl.ds(0, 15)], 9)
    left(r_sq.at[pl.ds(0, 15)], 10)
    left(r_v.at[pl.ds(0, 15)], 11)
    left(qk_all.at[pl.ds(0, 7)], 12)
    left(x3.at[pl.ds(0, 15)], 13)
    left(r_out.at[pl.ds(0, 31)], 14)
    left(x4.at[0, pl.ds(0, 15)], 15)
    left(x4.at[0], 22)

    arrived(r_up.at[pl.ds(0, 15)], 16)
    upward = total(r_up)
    stacked = jnp.concatenate([upward[:, tap * 64 : tap * 64 + 64] for tap in range(4)], axis=0)
    high = stacked.astype(BF16)
    low = (stacked - high.astype(F32)).astype(BF16)
    row = lax.broadcasted_iota(jnp.int32, (128, 128), 0)
    col = lax.broadcasted_iota(jnp.int32, (128, 128), 1)
    place = (col == 4 * lax.rem(row, 32) + lax.div(row, 32)).astype(F32).astype(BF16)
    out_ref[...] = (bytes_ref[...].astype(F32) + (dot00(high, place) + dot00(low, place))).astype(BF16)
    left(r_up.at[pl.ds(0, 15)], 16)


def per_device(
    byte_states, shorten_weight, norm_gain, qkv_weight, qk_gain, out_weight, up_weight, doc_lengths
):
    vmem = pl.BlockSpec(memory_space=pltpu.VMEM)
    hbm = pl.BlockSpec(memory_space=pl.ANY)

    def buf(*shape, dtype=BF16):
        return pltpu.VMEM(shape, dtype)

    return pl.pallas_call(
        kernel,
        out_shape=jax.ShapeDtypeStruct(byte_states.shape[::-1], BF16),
        in_specs=[hbm] * 8,
        out_specs=vmem,
        scratch_shapes=[
            buf(64, 128),
            buf(1, 128, dtype=F32),
            buf(2, 128, dtype=F32),
            pltpu.SMEM((6,), jnp.int32),
            buf(8, 32, ROWS, dtype=F32),
            buf(8, 32, ROWS),
            buf(8, 32, ROWS),
            buf(DEPTH, 32, ROWS),
            buf(2, DEPTH, 16, ROWS),
            buf(DEPTH, 16, ROWS),
            buf(2, DEPTH, 16, ROWS),
            buf(2, DEPTH, 1, 128, dtype=F32),
            buf(2, DEPTH, 16, 128, dtype=F32),
            buf(SLOTS, DEPTH, 4, 8, 128),
            buf(2, DEPTH, 2, 3, 16, 128),
            buf(SLOTS, DEPTH, 16, 128),
            buf(2, 2, DEPTH, 16, 256),
            buf(2, DEPTH, 2, 64, 64),
            buf(2, 2, DEPTH, 16, 256),
            buf(512, 512),
            buf(2, 512, 256),
            buf(256, 512),
            buf(512, 256),
            buf(SLOTS, 128, ROWS),
            buf(2, ROWS, 256),
            buf(2, 128, ROWS),
            buf(SLOTS, 128, ROWS),
            buf(2, ROWS, 256),
            buf(2, 128, dtype=F32),
            buf(PLANE, 16, ROWS),
            buf(PLANE // 2, 32, 256),
            buf(PLANE // 2, 16, ROWS),
            buf(PLANE, 16, ROWS),
            buf(PLANE // 2, 32, 256),
            buf(PLANE // 2, 2, 128, dtype=F32),
            buf(16, ROWS),
            buf(8, 32, 256),
            pltpu.SemaphoreType.DMA((23,)),
            pltpu.SemaphoreType.DMA((23,)),
            pltpu.SemaphoreType.DMA((11,)),
        ],
        compiler_params=pltpu.CompilerParams(
            collective_id=0, has_side_effects=True, vmem_limit_bytes=60 * 1024 * 1024
        ),
        cost_estimate=pl.CostEstimate(
            flops=2 * 256 * 256 * 4096, bytes_accessed=4 * 1024 * 1024, transcendentals=65536
        ),
    )(
        byte_states.T,
        shorten_weight.reshape(4, 2, DEPTH, 2, 8, 128),
        norm_gain.reshape(1, 128),
        qkv_weight.transpose(0, 1, 3, 2, 4).reshape(2, DEPTH, 2, 3, 16, 128),
        qk_gain,
        out_weight.reshape(2, DEPTH, 2, 16, 128),
        up_weight.reshape(2, DEPTH, 2, 64, 64),
        doc_lengths,
    ).T


def solution(mesh):
    placed = (
        P("mp", "ctx"),
        P(None, None, "mp", None, "ctx"),
        P("ctx"),
        P(None, "mp", None, None, "ctx"),
        P(),
        P(None, "mp", None, "ctx"),
        P(None, "mp", None, None, "ctx"),
        P(),
    )
    return jax.shard_map(
        per_device, mesh=mesh, in_specs=placed, out_specs=P("mp", "ctx"), check_vma=False
    )
```

```python
import jax
import jax.numpy as jnp
from jax import lax
from jax.experimental import pallas as pl
from jax.experimental.pallas import tpu as pltpu
from jax.sharding import PartitionSpec as P

F32 = jnp.float32
BF16 = jnp.bfloat16
MESH = pl.DeviceIdType.MESH
ROWS = 256
PLANE = 32
DEPTH = 16
SLOTS = 4


def dot00(a, b):
    return lax.dot_general(a, b, (((0,), (0,)), ((), ())), preferred_element_type=F32)


def kernel(
    bytes_hbm, wconv_hbm, gain_hbm, wqkv_hbm, qk_gain_hbm, wout_hbm, wup_hbm, docs_hbm,
    out_ref,
    bytes_ref, gain_ref, qk_gain_ref, docs_ref,
    p0_wide, p0_send, p0_recv,
    x1, x2, x3, x4,
    gains, column,
    wconv_in, wqkv_in, wout_in, wup_in, wup_raw, wup_own,
    wconv_t, wqk, wv_t, wout_t,
    s_conv, s_qk, s_v, s_out, s_up, s_sq,
    r_conv, r_qk, r_v, r_out, r_up, r_sq,
    short_own, qk_all,
    send_sem, recv_sem, local_sem,
):
    ctx = lax.axis_index("ctx")
    mp = lax.axis_index("mp")
    y_lo, z, core = lax.div(ctx, 32), lax.rem(lax.div(ctx, 2), DEPTH), lax.rem(ctx, 2)
    x = lax.rem(mp, 4)
    slot = y_lo * 2 + core
    me = mp * SLOTS + slot
    me_half = mp * 2 + y_lo

    lows = [1 - y_lo, y_lo]
    cores = [1 - core, core]
    columns = [lax.rem(x + step, 4) for step in (2, 1, 3, 0)]
    y_hi = lax.div(mp, 4)
    owners = [h * 4 + c for h in (1 - y_hi, y_hi) for c in columns]

    def depth_peer(i):
        far = 8 - (i + 1) // 2
        pz = lax.rem(z + (far if i % 2 else DEPTH - far), DEPTH)
        return (y_lo * 32 + pz * 2 + core, mp)

    def loop(count, body):
        for i in range(count):
            body(i)

    def put(src, dst, sem, device):
        pltpu.make_async_remote_copy(
            src_ref=src, dst_ref=dst, send_sem=send_sem.at[sem], recv_sem=recv_sem.at[sem],
            device_id=device, device_id_type=MESH,
        ).start()

    def arrived(view, sem):
        pltpu.make_async_copy(view, view, recv_sem.at[sem]).wait()

    def left(view, sem):
        pltpu.make_async_copy(view, view, send_sem.at[sem]).wait()

    def along_depth(buf, sem):
        loop(DEPTH - 1, lambda i: put(buf.at[z], buf.at[z], sem, depth_peer(i)))

    def to_slot(low, c, piece, dst, at, sem, itself):
        for owner in owners[: 7 if itself else 8]:
            put(piece(owner), dst.at[at], sem, (low * 32 + z * 2 + c, owner))

    def feature_sums(weights_t, block, sums, dst, sem):
        for low in lows:
            for c in cores:
                its_slot = low * 2 + c
                rows = pl.ds(pl.multiple_of(its_slot * 128, 128), 128)
                part = jnp.dot(weights_t[rows, :], block, preferred_element_type=F32)
                sums[its_slot] = part.astype(BF16)
                piece = feature_piece(sums, its_slot)
                to_slot(low, c, piece, dst, me, sem, low is y_lo and c is core)
        dst[me] = sums[slot, pl.ds(pl.multiple_of(mp * 16, 16), 16), :]

    def feature_piece(buf, at):
        return lambda m: buf.at[at, pl.ds(pl.multiple_of(m * 16, 16), 16), :]

    def row_piece(buf, at):
        return lambda m: buf.at[at, pl.ds(pl.multiple_of(m * 32, 32), 32), :]

    def to_half(piece, dst, sem):
        for low in lows:
            to_slot(low, core, piece(low), dst, me_half, sem, low is y_lo)

    def near(i):
        far = 4 - i // 2
        return shifted(DEPTH - far if i % 2 else far)

    def shifted(step):
        return lax.rem(z + step, DEPTH)

    def at_depth(pz):
        return (y_lo * 32 + pz * 2 + core, mp)

    def same_slot(i):
        return lax.rem(mp + 1 + i, 8)

    def regroup_peer(i):
        p_lo = lax.rem(y_lo + (i + 1) // 2, 2)
        p_core = lax.rem(core + i + 1, 2)
        return p_lo, p_core, (p_lo * 32 + z * 2 + p_core, mp)

    barrier = pltpu.get_barrier_semaphore()

    def greet(device):
        pl.semaphore_signal(barrier, inc=1, device_id=device, device_id_type=MESH)

    loop(8, lambda i: greet(at_depth(near(i))))
    loop(7, lambda i: greet((ctx, same_slot(i))))
    loop(3, lambda i: greet(regroup_peer(i)[2]))

    small = []
    for i, (src, dst) in enumerate(
        ((bytes_hbm, bytes_ref), (gain_hbm, gain_ref), (qk_gain_hbm, qk_gain_ref), (docs_hbm, docs_ref))
    ):
        small.append(pltpu.make_async_copy(src, dst, local_sem.at[7 + i]))
    for copy in small:
        copy.start()

    own = []
    for tap in range(4):
        own.append((wconv_hbm.at[tap, y_lo, :, core], wconv_in.at[slot, :, tap]))
    own.append((wqkv_hbm.at[y_lo], wqkv_in.at[y_lo]))
    own.append((wout_hbm.at[y_lo, :, core], wout_in.at[slot]))
    own = [pltpu.make_async_copy(a, b, local_sem.at[i]) for i, (a, b) in enumerate(own)]
    for copy in own:
        copy.start()
    raw_up = pltpu.make_async_copy(wup_hbm, wup_raw, local_sem.at[6])
    raw_up.start()

    for copy in small:
        copy.wait()
    local = bytes_ref[...]
    row = lax.broadcasted_iota(jnp.int32, (128, ROWS), 0)
    col = lax.broadcasted_iota(jnp.int32, (128, ROWS), 1)
    for tap in range(4):
        pick = (row + mp * 128 == 4 * col + (tap - 3)).astype(F32).astype(BF16)
        placed = jnp.dot(local, pick, preferred_element_type=F32)
        for m in range(8):
            p0_wide[m, tap * 8 : tap * 8 + 8, :] = placed[m * 8 : m * 8 + 8, :]
    p0_send[...] = p0_wide[...].astype(BF16)
    p0_recv[mp] = p0_send[mp]

    pl.semaphore_wait(barrier, 18)

    def trade(i):
        other = same_slot(i)
        put(p0_send.at[other], p0_recv.at[mp], 0, (ctx, other))

    loop(7, trade)

    across = ((1 - y_lo) * 32 + z * 2 + core, mp)
    twin = (ctx + 1 - 2 * core, mp)
    peers = [regroup_peer(jnp.int32(i)) for i in range(3)]
    for p_lo, p_core, device in peers:
        for tap in range(4):
            put(wconv_hbm.at[tap, p_lo, :, p_core], wconv_in.at[slot, :, tap], 1, device)
    arrived(p0_recv.at[pl.ds(0, 7)], 0)
    block = p0_recv[0].astype(F32)
    for m in range(1, 8):
        block = block + p0_recv[m].astype(F32)
    x1[z] = block.astype(BF16)

    def spread(block, device, sem):
        put(x1.at[block], x1.at[block], sem, at_depth(device))

    ahead, behind = shifted(4), shifted(DEPTH - 4)
    spread(z, ahead, 5)
    spread(z, behind, 17)
    loop(6, lambda i: spread(z, near(i + 2), 18))
    put(wqkv_hbm.at[1 - y_lo], wqkv_in.at[y_lo], 2, across)
    arrived(x1.at[behind], 5)
    loop(4, lambda i: spread(behind, shifted(4 - i), 19))
    arrived(x1.at[ahead], 17)
    loop(3, lambda i: spread(ahead, shifted(DEPTH - 3 + i), 19))

    for copy in own[:4]:
        copy.wait()
    arrived(wconv_in.at[pl.ds(0, 3)], 1)
    for s in range(SLOTS):
        flat = wconv_in[s].astype(F32).reshape(DEPTH * 32, 128)
        wconv_t[s * 128 : s * 128 + 128, :] = flat.T.astype(BF16)

    arrived(x1.at[pl.ds(0, 6)], 18)
    arrived(x1.at[pl.ds(0, 7)], 19)
    feature_sums(wconv_t, x1[...].reshape(DEPTH * 32, ROWS), s_conv, r_conv, 7)
    loop(DEPTH - 1, lambda i: put(gain_ref, gains.at[core, z], 6, depth_peer(i)))

    raw_up.wait()
    row = lax.broadcasted_iota(jnp.int32, (256, 256), 0)
    col = lax.broadcasted_iota(jnp.int32, (256, 256), 1)
    sort = (col == 4 * lax.rem(row, 64) + lax.div(row, 64)).astype(F32).astype(BF16)
    for lo, c, quarter in ((a, b, q) for a in range(2) for b in range(2) for q in range(4)):
        rows = wup_raw[lo, quarter * 4 : quarter * 4 + 4, c].reshape(256, 64)
        taps = jnp.dot(sort, rows, preferred_element_type=F32).astype(BF16)
        wup_own[lo, c, quarter * 4 : quarter * 4 + 4] = jnp.concatenate(
            [taps[tap * 64 : tap * 64 + 64] for tap in range(4)], axis=1
        ).reshape(4, 16, 256)
    wup_in[y_lo] = wup_own[y_lo]

    def total(buf):
        acc = buf[0].astype(F32)
        for i in range(1, buf.shape[0]):
            acc = acc + buf[i].astype(F32)
        return acc

    arrived(r_conv.at[pl.ds(0, 31)], 7)
    short = total(r_conv).astype(BF16)
    short_own[...] = short
    x2[core, z] = short
    along_depth(x2.at[core], 8)
    for p_lo, p_core, device in peers:
        put(wout_hbm.at[p_lo, :, p_core], wout_in.at[slot], 3, device)

    own[4].wait()
    arrived(wqkv_in.at[0], 2)
    arrived(gains.at[0, pl.ds(0, 15)], 6)
    gains[core, z] = gain_ref[...]
    put(gains.at[core], gains.at[core], 20, twin)
    arrived(gains.at[0], 20)
    lane = lax.broadcasted_iota(jnp.int32, (16, 128), 1)
    feat = lax.broadcasted_iota(jnp.int32, (16, 128), 0)
    for c in range(2):
        for d in range(DEPTH):
            mine = jnp.where(lane == feat + mp * 16, gains[c, d], 0.0)
            column[c, d] = jnp.broadcast_to(jnp.sum(mine, axis=1, keepdims=True), (16, 128))
    for c in range(2):
        gain_rows = column[c].reshape(256, 128)
        for s in range(2):
            for kind in range(2):
                w = wqkv_in[s, :, c, kind].reshape(256, 128).astype(F32) * gain_rows
                at = kind * 128
                wqk[s, c * 256 : c * 256 + 256, at : at + 128] = w.astype(BF16)
            w = wqkv_in[s, :, c, 2].reshape(256, 128).astype(F32) * gain_rows
            wv_t[s * 128 : s * 128 + 128, c * 256 : c * 256 + 256] = w.T.astype(BF16)

    arrived(x2.at[0, pl.ds(0, 15)], 8)
    put(x2.at[core], x2.at[core], 21, twin)
    arrived(x2.at[0], 21)
    gathered = x2[...].reshape(512, ROWS)
    for low in lows:
        s_qk[low] = dot00(gathered, wqk[low]).astype(BF16)
        to_slot(low, core, row_piece(s_qk, low), r_qk, me_half, 9, low is y_lo)
    wide = gathered.astype(F32)
    squares = jnp.sum(wide * wide, axis=0, keepdims=True)
    s_sq[0:1, :] = squares[:, :128]
    s_sq[1:2, :] = squares[:, 128:]
    r_sq[me_half] = s_sq[...]
    to_half(lambda low: lambda m: s_sq, r_sq, 10)
    v = jnp.dot(wv_t[...], gathered, preferred_element_type=F32)
    s_v[...] = v.astype(BF16).reshape(2, 128, ROWS)
    to_half(lambda low: feature_piece(s_v, low), r_v, 11)
    r_qk[me_half] = s_qk[y_lo, pl.ds(pl.multiple_of(mp * 32, 32), 32), :]
    r_v[me_half] = s_v[y_lo, pl.ds(pl.multiple_of(mp * 16, 16), 16), :]

    own[5].wait()
    arrived(wout_in.at[pl.ds(0, 3)], 3)
    for s in range(SLOTS):
        wout_t[s * 128 : s * 128 + 128, :] = wout_in[s].reshape(256, 128).astype(F32).T.astype(BF16)

    key = lax.broadcasted_iota(jnp.int32, (ROWS, ROWS), 0)
    query = lax.broadcasted_iota(jnp.int32, (ROWS, ROWS), 1)
    key_pos = lax.broadcasted_iota(jnp.int32, (ROWS, 1), 0) * 4
    query_pos = lax.broadcasted_iota(jnp.int32, (1, ROWS), 1) * 4
    key_seg = jnp.zeros((ROWS, 1), jnp.int32)
    query_seg = jnp.zeros((1, ROWS), jnp.int32)
    end = jnp.int32(0)
    for d in range(docs_ref.shape[0]):
        end = end + docs_ref[d]
        key_seg = key_seg + (key_pos >= end).astype(jnp.int32)
        query_seg = query_seg + (query_pos >= end).astype(jnp.int32)
    allowed = (key <= query) & (key_seg == query_seg)

    arrived(r_sq.at[pl.ds(0, 15)], 10)
    mean = jnp.sum(r_sq[...], axis=0) / 8192.0
    inverse = lax.rsqrt(mean + 1e-06)
    inverse = jnp.concatenate([inverse[0:1, :], inverse[1:2, :]], axis=1)
    at_row = lax.broadcasted_iota(jnp.int32, (32, ROWS), 0) + mp * 32
    at_lane = lax.broadcasted_iota(jnp.int32, (32, ROWS), 1)
    row_inverse = jnp.sum(jnp.where(at_row == at_lane, inverse, 0.0), axis=1, keepdims=True)

    arrived(r_qk.at[pl.ds(0, 15)], 9)
    both = total(r_qk) * row_inverse
    for kind in range(2):
        part = both[:, kind * 128 : kind * 128 + 128]
        scale = lax.rsqrt(jnp.mean(part * part, axis=1, keepdims=True) + 1e-06)
        qk_all[mp, :, kind * 128 : kind * 128 + 128] = (
            part * scale * qk_gain_ref[kind : kind + 1, :]
        ).astype(BF16)

    def share(i):
        other = same_slot(i)
        put(qk_all.at[mp], qk_all.at[mp], 12, (ctx, other))

    loop(7, share)

    arrived(r_v.at[pl.ds(0, 15)], 11)
    values = (total(r_v) * inverse).astype(BF16)

    arrived(qk_all.at[pl.ds(0, 7)], 12)
    queries = qk_all[:, :, 0:128].reshape(ROWS, 128)
    keys = qk_all[:, :, 128:256].reshape(ROWS, 128)
    scores = lax.dot_general(
        keys, queries, (((1,), (1,)), ((), ())), preferred_element_type=F32
    ) * (1.0 / 128**0.5)
    weights = jnp.where(allowed, jnp.exp(scores), 0.0)
    denominator = jnp.sum(weights, axis=0, keepdims=True)
    numerator = jnp.dot(values, weights.astype(BF16), preferred_element_type=F32)
    x3[z] = (numerator / denominator).astype(BF16)
    along_depth(x3, 13)
    put(wup_own.at[1 - y_lo], wup_in.at[y_lo], 4, across)

    arrived(wup_in.at[0], 4)

    arrived(x3.at[pl.ds(0, 15)], 13)
    feature_sums(wout_t, x3[...].reshape(256, ROWS), s_out, r_out, 14)
    arrived(r_out.at[pl.ds(0, 31)], 14)
    x4[core, z] = (short_own[...].astype(F32) + total(r_out)).astype(BF16)
    along_depth(x4.at[core], 15)
    arrived(x4.at[0, pl.ds(0, 15)], 15)
    put(x4.at[core], x4.at[core], 22, twin)
    rows = x4[core].reshape(256, ROWS)
    begun = [dot00(rows, wup_in[low, core].reshape(256, 256)) for low in lows]
    arrived(x4.at[0], 22)
    rows = x4[1 - core].reshape(256, ROWS)
    for low, part in zip(lows, begun):
        part = part + dot00(rows, wup_in[low, 1 - core].reshape(256, 256))
        s_up[low] = part.astype(BF16)
        to_slot(low, core, row_piece(s_up, low), r_up, me_half, 16, low is y_lo)
    r_up[me_half] = s_up[y_lo, pl.ds(pl.multiple_of(mp * 32, 32), 32), :]

    left(p0_recv.at[pl.ds(0, 7)], 0)
    left(wconv_in.at[pl.ds(0, 3)], 1)
    left(wqkv_in.at[0], 2)
    left(wout_in.at[pl.ds(0, 3)], 3)
    left(wup_in.at[0], 4)
    left(x1.at[0], 5)
    left(x1.at[0], 17)
    left(x1.at[pl.ds(0, 6)], 18)
    left(x1.at[pl.ds(0, 7)], 19)
    left(gains.at[0, pl.ds(0, 15)], 6)
    left(gains.at[0], 20)
    left(r_conv.at[pl.ds(0, 31)], 7)
    left(x2.at[0, pl.ds(0, 15)], 8)
    left(x2.at[0], 21)
    left(r_qk.at[pl.ds(0, 15)], 9)
    left(r_sq.at[pl.ds(0, 15)], 10)
    left(r_v.at[pl.ds(0, 15)], 11)
    left(qk_all.at[pl.ds(0, 7)], 12)
    left(x3.at[pl.ds(0, 15)], 13)
    left(r_out.at[pl.ds(0, 31)], 14)
    left(x4.at[0, pl.ds(0, 15)], 15)
    left(x4.at[0], 22)

    arrived(r_up.at[pl.ds(0, 15)], 16)
    upward = total(r_up)
    stacked = jnp.concatenate([upward[:, tap * 64 : tap * 64 + 64] for tap in range(4)], axis=0)
    high = stacked.astype(BF16)
    low = (stacked - high.astype(F32)).astype(BF16)
    row = lax.broadcasted_iota(jnp.int32, (128, 128), 0)
    col = lax.broadcasted_iota(jnp.int32, (128, 128), 1)
    place = (col == 4 * lax.rem(row, 32) + lax.div(row, 32)).astype(F32).astype(BF16)
    out_ref[...] = (bytes_ref[...].astype(F32) + (dot00(high, place) + dot00(low, place))).astype(BF16)
    left(r_up.at[pl.ds(0, 15)], 16)


def per_device(
    byte_states, shorten_weight, norm_gain, qkv_weight, qk_gain, out_weight, up_weight, doc_lengths
):
    vmem = pl.BlockSpec(memory_space=pltpu.VMEM)
    hbm = pl.BlockSpec(memory_space=pl.ANY)

    def buf(*shape, dtype=BF16):
        return pltpu.VMEM(shape, dtype)

    return pl.pallas_call(
        kernel,
        out_shape=jax.ShapeDtypeStruct(byte_states.shape[::-1], BF16),
        in_specs=[hbm] * 8,
        out_specs=vmem,
        scratch_shapes=[
            buf(64, 128),
            buf(1, 128, dtype=F32),
            buf(2, 128, dtype=F32),
            pltpu.SMEM((6,), jnp.int32),
            buf(8, 32, ROWS, dtype=F32),
            buf(8, 32, ROWS),
            buf(8, 32, ROWS),
            buf(DEPTH, 32, ROWS),
            buf(2, DEPTH, 16, ROWS),
            buf(DEPTH, 16, ROWS),
            buf(2, DEPTH, 16, ROWS),
            buf(2, DEPTH, 1, 128, dtype=F32),
            buf(2, DEPTH, 16, 128, dtype=F32),
            buf(SLOTS, DEPTH, 4, 8, 128),
            buf(2, DEPTH, 2, 3, 16, 128),
            buf(SLOTS, DEPTH, 16, 128),
            buf(2, 2, DEPTH, 16, 256),
            buf(2, DEPTH, 2, 64, 64),
            buf(2, 2, DEPTH, 16, 256),
            buf(512, 512),
            buf(2, 512, 256),
            buf(256, 512),
            buf(512, 256),
            buf(SLOTS, 128, ROWS),
            buf(2, ROWS, 256),
            buf(2, 128, ROWS),
            buf(SLOTS, 128, ROWS),
            buf(2, ROWS, 256),
            buf(2, 128, dtype=F32),
            buf(PLANE, 16, ROWS),
            buf(PLANE // 2, 32, 256),
            buf(PLANE // 2, 16, ROWS),
            buf(PLANE, 16, ROWS),
            buf(PLANE // 2, 32, 256),
            buf(PLANE // 2, 2, 128, dtype=F32),
            buf(16, ROWS),
            buf(8, 32, 256),
            pltpu.SemaphoreType.DMA((23,)),
            pltpu.SemaphoreType.DMA((23,)),
            pltpu.SemaphoreType.DMA((11,)),
        ],
        compiler_params=pltpu.CompilerParams(
            collective_id=0, has_side_effects=True, vmem_limit_bytes=60 * 1024 * 1024
        ),
        cost_estimate=pl.CostEstimate(
            flops=2 * 256 * 256 * 4096, bytes_accessed=4 * 1024 * 1024, transcendentals=65536
        ),
    )(
        byte_states.T,
        shorten_weight.reshape(4, 2, DEPTH, 2, 8, 128),
        norm_gain.reshape(1, 128),
        qkv_weight.transpose(0, 1, 3, 2, 4).reshape(2, DEPTH, 2, 3, 16, 128),
        qk_gain,
        out_weight.reshape(2, DEPTH, 2, 16, 128),
        up_weight.reshape(2, DEPTH, 2, 64, 64),
        doc_lengths,
    ).T


def solution(mesh):
    placed = (
        P("mp", "ctx"),
        P(None, None, "mp", None, "ctx"),
        P("ctx"),
        P(None, "mp", None, None, "ctx"),
        P(),
        P(None, "mp", None, "ctx"),
        P(None, "mp", None, None, "ctx"),
        P(),
    )
    return jax.shard_map(
        per_device, mesh=mesh, in_specs=placed, out_specs=P("mp", "ctx"), check_vma=False
    )
```
